128 devices in a mesh: key: 16 (over y_lo, x, core), limb: 8 (over z, y_hi).
Axes of the slice: x: 4, y: 4 (y_hi: 2, y_lo: 2; y = y_hi * 2 + y_lo), z: 4, core: 2. Of those that a mesh axis runs over, the one named last changes fastest.
Arguments:
- cipher: float32 [16, 2, 24, 32768], P('key', None, 'limb'), may hold values from -6 to 6
- key_main: bfloat16 [16, 2, 3, 24, 32768], P('key', None, None, 'limb'), may hold values from -4 to 4
- key_special: bfloat16 [16, 2, 3, 8, 32768], P('key', None, None, 'limb'), may hold values from -4 to 4
- diag_main: bfloat16 [16, 24, 32768], P('key', 'limb'), may hold values from -5 to 5
- diag_special: bfloat16 [16, 8, 32768], P('key', 'limb'), may hold values from -5 to 5
- perms: int32 [16, 32768], P('key'), may hold values from 0 to 32767, each once within a row
- tw_exp: int32 [32], replicated, may hold values from 1 to 32767
- up_conv: float32 [24, 32], replicated, may hold values from -2 to 2
- down_conv: float32 [8, 24], replicated, may hold values from -2 to 2
Outputs:
- rotated: float32 [16, 2, 24, 32768], P('key', None, 'limb')
The draws below stay inside these ranges and needn't reach their ends.
Inputs may be any that keep to these rules, and one draw needn't show every extreme that they name: Each row of perms holds every coefficient position once.
All inputs are finite; a program needn't handle non-finite values.
Results may differ from the reference program's by a relative error of at most 0.0003.
Values may be sent and summed in bfloat16 or wider, within the bound.
No kernel may reach another device: no remote copies, remote signals or barrier semaphores. Data moves between devices by JAX's collectives and lax.ppermute only.
A program may use at most 640 MiB of HBM per device.

```python
import math
import jax
import jax.numpy as jnp
from jax import lax

NRING = 32768
A = 128
Q = 24
K = 8
DNUM = 3
ROTS = 2
CTS = 16


def plant(result, own_key, smallest, top_value):
    shape = result.shape
    place = [jax.random.randint(jax.random.fold_in(own_key, axis), (), 0, shape[axis]) for axis in range(len(shape))]
    result = result.at[tuple(place)].set(smallest)
    longest = shape.index(max(shape))
    place[longest] = (place[longest] + 1) % shape[longest]
    return result.at[tuple(place)].set(top_value)


def steps_of(key, shape, shards, least, largest):
    gain = 1.0
    for dim, blocks in shards:
        heights = jax.random.uniform(jax.random.fold_in(jax.random.fold_in(key, 6), dim), (blocks,), jnp.float32, least / len(shards), largest / len(shards))
        gain = gain * jnp.repeat(jnp.exp(heights), shape[dim] // blocks).reshape((-1,) + (1,) * (len(shape) - 1 - dim))
    return gain


def gaussian(own_key, shape, spread, most, cuts=(), kind=jnp.bfloat16):
    values = jax.random.normal(own_key, shape, jnp.float32) * spread
    if len(cuts) > 0:
        values = steps_of(own_key, shape, cuts, -0.22, 0.18) * values
    return jnp.clip(values, min=-most, max=most).astype(kind)


def setup_inputs(seed: int = 0) -> dict:
    seeds = jax.random.split(jax.random.key(seed), 10)
    cipher = gaussian(seeds[0], (CTS, 2, Q, NRING), 1.0, 6.0, ((0, 16), (2, 8)), jnp.float32)
    key_main = gaussian(seeds[1], (CTS, 2, DNUM, Q, NRING), 0.6, 4.0, ((0, 16), (3, 8)))
    key_special = gaussian(seeds[2], (CTS, 2, DNUM, K, NRING), 0.6, 4.0, ((0, 16), (3, 8)))
    diag_main = gaussian(seeds[3], (CTS, Q, NRING), 1.0, 5.0, ((0, 16), (1, 8)))
    diag_special = gaussian(seeds[4], (CTS, K, NRING), 1.0, 5.0, ((0, 16), (1, 8)))
    perms = jax.vmap(lambda own: jax.random.permutation(own, NRING))(jax.random.split(seeds[5], CTS)).reshape((CTS, NRING)).astype(jnp.int32)
    tw_exp = plant(jax.random.randint(seeds[6], (Q + K,), 1, NRING), jax.random.fold_in(seeds[6], 1), 1, NRING - 1).astype(jnp.int32)
    up_conv = gaussian(seeds[7], (Q, Q + K), (Q // DNUM) ** -0.5, 2.0, (), jnp.float32)
    down_conv = gaussian(seeds[8], (K, Q), K ** -0.5, 2.0, (), jnp.float32)
    return dict(cipher=cipher, key_main=key_main, key_special=key_special, diag_main=diag_main, diag_special=diag_special, perms=perms, tw_exp=tw_exp, up_conv=up_conv, down_conv=down_conv)


HIGHEST_PRECISION = lax.Precision.HIGHEST

def hartley(extent):
    indices = jnp.arange(extent, dtype=jnp.int32)
    phases = indices[:, None] * indices[None, :] % extent
    angles = phases.astype(jnp.float32) * (2.0 * math.pi / extent)
    return (jnp.cos(angles) + jnp.sin(angles)) / math.sqrt(extent)

def twiddle(exponents, row_count, col_count, length):
    row_index = jnp.arange(row_count, dtype=jnp.int32)
    col_index = jnp.arange(col_count, dtype=jnp.int32)
    product = row_index[:, None] * col_index[None, :] % length
    phases = product[None, :, :] * exponents.astype(jnp.int32)[:, None, None] % length
    angles = phases.astype(jnp.float32) * (2.0 * math.pi / length)
    return 1.0 + 0.5 * jnp.cos(angles)

def forward(values, exponents, row_count):
    layout = values.shape
    length = layout[-1]
    col_count = length // row_count
    blocks = values.reshape(layout[:-1] + (row_count, col_count)) * twiddle(exponents, row_count, col_count, length)
    halfway = jnp.einsum('ia,...ab->...ib', hartley(row_count), blocks, precision=HIGHEST_PRECISION)
    finished = jnp.einsum('...ib,bj->...ij', halfway, hartley(col_count), precision=HIGHEST_PRECISION)
    return finished.reshape(layout)

def inverse(values, exponents, row_count):
    layout = values.shape
    length = layout[-1]
    col_count = length // row_count
    blocks = values.reshape(layout[:-1] + (row_count, col_count))
    halfway = jnp.einsum('ia,...ab->...ib', hartley(row_count), blocks, precision=HIGHEST_PRECISION)
    finished = jnp.einsum('...ib,bj->...ij', halfway, hartley(col_count), precision=HIGHEST_PRECISION)
    finished = finished / twiddle(exponents, row_count, col_count, length)
    return finished.reshape(layout)

def digit_weights(up_conv, digit_count):
    limb_count = up_conv.shape[0]
    group_of = jnp.arange(limb_count, dtype=jnp.int32) * digit_count // limb_count
    members = (group_of[:, None] == jnp.arange(digit_count, dtype=jnp.int32)[None, :]).astype(jnp.float32)
    return members[:, :, None] * up_conv[:, None, :]

def reference(cipher, key_main, key_special, diag_main, diag_special, perms, tw_exp, up_conv, down_conv):
    weights = digit_weights(up_conv, DNUM)
    exps_main = tw_exp[:Q]
    exps_spec = tw_exp[Q:]

    def single(item):
        cipher_one, position = item
        coefficients = inverse(cipher_one[1], exps_main, A)
        raised = jnp.einsum('ln,ldm->dmn', coefficients, weights, precision=HIGHEST_PRECISION)
        extended = forward(raised, tw_exp, A)
        summed = jnp.zeros((2, Q + K, NRING), jnp.float32)
        for rotation in range(ROTS):
            owner = (position + rotation) % CTS
            mapping = perms[owner]
            permuted = jnp.take(extended, mapping, axis=2)
            base_part = jnp.take(cipher_one[0], mapping, axis=1)
            key_rows = jnp.concatenate([key_main[owner], key_special[owner]], axis=2).astype(jnp.float32)
            switched = lax.optimization_barrier(jnp.sum(key_rows * permuted[None], axis=1))
            lifted = jnp.concatenate([base_part, jnp.zeros((K, NRING), jnp.float32)], axis=0)
            switched = switched + jnp.stack([lifted, jnp.zeros_like(lifted)])
            diagonal = jnp.concatenate([diag_main[owner], diag_special[owner]], axis=0).astype(jnp.float32)
            summed = summed + diagonal[None] * switched
        lowered = inverse(summed[:, Q:], exps_spec, A)
        returned = jnp.einsum('pkn,kl->pln', lowered, down_conv, precision=HIGHEST_PRECISION)
        return summed[:, :Q] - forward(returned, exps_main, A)
    return lax.map(single, (cipher, jnp.arange(CTS, dtype=jnp.int32)))
```

```python
import functools
import math

import jax
import jax.numpy as jnp
import numpy as np
from jax import lax
from jax.experimental import pallas as pl
from jax.experimental.pallas import tpu as pltpu
from jax.sharding import PartitionSpec as P

A = 128
B = 256
NRING = A * B
DNUM = 3
LIMBS = 8
JS = 4
CHUNK = A // LIMBS
HIGHEST = lax.Precision.HIGHEST
MIB = 1 << 20

VMEM = pl.BlockSpec(memory_space=pltpu.VMEM)
SMEM = pl.BlockSpec(memory_space=pltpu.SMEM)


def hartley(extent):
    indices = np.arange(extent)
    angles = (indices[:, None] * indices[None, :] % extent) * (2.0 * math.pi / extent)
    return ((np.cos(angles) + np.sin(angles)) / math.sqrt(extent)).astype(np.float32)


def twiddle(exponents):
    product = jnp.arange(A, dtype=jnp.int32)[:, None] * jnp.arange(B, dtype=jnp.int32)[None, :] % NRING
    phases = product[None, :, :] * exponents[:, None, None] % NRING
    return 1.0 + 0.5 * jnp.cos(phases.astype(jnp.float32) * (2.0 * math.pi / NRING))


def params(mib):
    return pltpu.CompilerParams(vmem_limit_bytes=mib * MIB)


def both_sides(h_a, block, h_b):
    half = jnp.dot(h_a, block, precision=HIGHEST, preferred_element_type=jnp.float32)
    return jnp.dot(half, h_b, precision=HIGHEST, preferred_element_type=jnp.float32)


def inverse_kernel(cipher_ref, tw_ref, ha_ref, hb_ref, out_ref, x_ref):
    def spread(step, _):
        rows = [cipher_ref[0, 0, :, pl.ds(pl.multiple_of((step * 8 + k) * B, B), B)] for k in range(8)]
        for limb in range(JS - 1):
            x_ref[limb, pl.ds(pl.multiple_of(step * 8, 8), 8), :] = jnp.concatenate([row[limb : limb + 1] for row in rows], axis=0)
        return 0

    lax.fori_loop(0, A // 8, spread, 0)
    for limb in range(JS - 1):
        done = both_sides(ha_ref[...], x_ref[limb], hb_ref[...]) / tw_ref[limb]
        for to in range(LIMBS):
            out_ref[to, limb * CHUNK : (limb + 1) * CHUNK, :] = done[to * CHUNK : (to + 1) * CHUNK]


def raise_kernel(up_ref, x_ref, out_ref):
    def body(to, _):
        for digit in range(DNUM):
            for j in range(JS):
                m = to * (JS - 1) + j if j < JS - 1 else LIMBS * (JS - 1) + to
                total = None
                for limb in range(digit * LIMBS, (digit + 1) * LIMBS):
                    at = limb % (JS - 1) * CHUNK
                    term = up_ref[limb, m] * x_ref[limb // (JS - 1), at : at + CHUNK, :]
                    total = term if total is None else total + term
                at = (digit * JS + j) * CHUNK
                out_ref[to, at : at + CHUNK, :] = total
        return 0

    lax.fori_loop(0, LIMBS, body, 0)


def pack_kernel(km_ref, ks_ref, dm_ref, ds_ref, out_ref, rows_ref):
    for p in range(2):
        for digit in range(DNUM):
            at = p * 16 + digit * JS
            rows_ref[at : at + JS - 1, :] = km_ref[0, p, digit].astype(jnp.float32)
            rows_ref[at + JS - 1 : at + JS, :] = ks_ref[0, p, digit].astype(jnp.float32)
        at = p * 16 + DNUM * JS
        rows_ref[at : at + JS - 1, :] = dm_ref[0].astype(jnp.float32)
        rows_ref[at + JS - 1 : at + JS, :] = ds_ref[0].astype(jnp.float32)
    out_ref[...] = rows_ref[...].astype(jnp.bfloat16)


def switch_kernel(
    idx0_ref, idx1_ref, x_ref, base_ref, tw_ref, ha_ref, hb_ref, k0_ref, k1_ref,
    sum_ref, low_ref, rows_ref, ext_ref, got0_ref, got1_ref, spec_ref,
):
    channels = DNUM * JS
    for ch in range(channels):
        at = ch * CHUNK
        block = jnp.concatenate([x_ref[src, at : at + CHUNK, :] for src in range(LIMBS)], axis=0)
        done = both_sides(ha_ref[...], block * tw_ref[ch % JS], hb_ref[...])
        rows_ref[0, pl.ds(ch, A, stride=16), :] = done[:, :128]
        rows_ref[1, pl.ds(ch, A, stride=16), :] = done[:, 128:]

    def first(i, _):
        for half in range(2):
            lanes = pl.ds(pl.multiple_of(i * B + half * 128, 128), 128)
            rows_ref[half, pl.ds(pl.multiple_of(i * 16 + 8, 8) + 4, 3), :] = base_ref[0, 0, :, lanes]
            rows_ref[half, pl.ds(pl.multiple_of(i * 16 + 8, 8) + 7, 1), :] = jnp.zeros((1, 128), jnp.float32)
        return 0

    lax.fori_loop(0, A, first, 0)

    def turn(step, _):
        for k in range(4):
            i = step * 4 + k
            for half in range(2):
                part = rows_ref[half, pl.ds(pl.multiple_of(i * 16, 16), 16), :]
                ext_ref[pl.ds(pl.multiple_of(i * B + half * 128, 128), 128), :] = jnp.concatenate([part] * 8, axis=0).T
        return 0

    lax.fori_loop(0, A // 4, turn, 0)

    group = lax.broadcasted_iota(jnp.int32, (1, 128), 1) // 16

    def gather(idx_ref, got_ref):
        def body(step, _):
            blk = step // 8
            r0 = step % 8 * 16
            for r in range(16):
                row = None
                for g in range(8):
                    one = ext_ref[pl.ds(idx_ref[blk * 1024 + r0 + (g * 128 + r)], 1), :]
                    row = one if row is None else jnp.where(group == g, one, row)
                got_ref[step, r : r + 1, :] = row
            return 0

        lax.fori_loop(0, NRING // 128, body, 0)

    gather(idx0_ref, got0_ref)
    gather(idx1_ref, got1_ref)

    sub = lax.broadcasted_iota(jnp.int32, (8, 128), 0)
    low_half = sub < JS
    base_gain = jnp.where((sub >= JS) & (sub < 2 * JS - 1), 1.0, 0.0).astype(jnp.float32)

    def combine(step, _):
        lines = [[[], []], [[], []]]
        for k in range(16):
            blk, g = step * 2 + k // 8, k % 8
            if g == 0:
                at8 = pl.ds(blk * 8, 8)
                turned = [ref[at8].reshape(128, 128).T for ref in (got0_ref, got1_ref)]
            lanes = pl.ds(pl.multiple_of(step * 2048 + k * 128, 128), 128)
            sums = [None, None]
            for s, k_ref in enumerate((k0_ref, k1_ref)):
                keys = k_ref[:, lanes].astype(jnp.float32)
                upper = turned[s][g * 16 : g * 16 + 8]
                lower = turned[s][g * 16 + 8 : g * 16 + 16]
                tail = keys[8:16]
                diag = jnp.where(low_half, jnp.roll(tail, JS, axis=0), tail)
                for p in range(2):
                    gain = jnp.where(low_half, keys[p * 16 + 8 : p * 16 + 16], base_gain if p == 0 else 0.0)
                    part = diag * (keys[p * 16 : p * 16 + 8] * upper + gain * lower)
                    sums[p] = part if sums[p] is None else sums[p] + part
            folded = [value + jnp.roll(value, JS, axis=0) for value in sums]
            both = jnp.where(low_half, folded[0], folded[1])
            sum_ref[:, lanes] = both
            for p in range(2):
                lines[p][k % 2].append(both[p * JS + JS - 1 : p * JS + JS])
        at = pl.ds(pl.multiple_of(step * 8, 8), 8)
        for p in range(2):
            for half in range(2):
                spec_ref[p, at, half * 128 : (half + 1) * 128] = jnp.concatenate(lines[p][half], axis=0)
        return 0

    lax.fori_loop(0, NRING // 2048, combine, 0)

    for p in range(2):
        done = both_sides(ha_ref[...], spec_ref[p], hb_ref[...]) / tw_ref[JS - 1]
        for to in range(LIMBS):
            low_ref[to, p * CHUNK : (p + 1) * CHUNK, :] = done[to * CHUNK : (to + 1) * CHUNK]


def lower_kernel(down_ref, x_ref, out_ref):
    def body(to, _):
        for p in range(2):
            for j in range(JS - 1):
                total = None
                for k in range(LIMBS):
                    term = down_ref[k, to * (JS - 1) + j] * x_ref[k, p * CHUNK : (p + 1) * CHUNK, :]
                    total = term if total is None else total + term
                at = (p * (JS - 1) + j) * CHUNK
                out_ref[to, at : at + CHUNK, :] = total
        return 0

    lax.fori_loop(0, LIMBS, body, 0)


def finish_kernel(x_ref, sum_ref, tw_ref, ha_ref, hb_ref, out_ref, rows_ref):
    for p in range(2):
        for j in range(JS - 1):
            at = (p * (JS - 1) + j) * CHUNK
            block = jnp.concatenate([x_ref[src, at : at + CHUNK, :] for src in range(LIMBS)], axis=0)
            done = both_sides(ha_ref[...], block * tw_ref[j], hb_ref[...])
            rows_ref[0, pl.ds(p * JS + j, A, stride=8), :] = done[:, :128]
            rows_ref[1, pl.ds(p * JS + j, A, stride=8), :] = done[:, 128:]

    def body(i, _):
        for half in range(2):
            lanes = pl.ds(pl.multiple_of(i * B + half * 128, 128), 128)
            rest = sum_ref[:, lanes] - rows_ref[half, pl.ds(pl.multiple_of(i * 8, 8), 8), :]
            for p in range(2):
                out_ref[0, p, :, lanes] = rest[p * JS : p * JS + JS - 1]
        return 0

    lax.fori_loop(0, A, body, 0)


def exchange(value):
    return lax.all_to_all(value, "limb", split_axis=0, concat_axis=0, tiled=True)


def f32(*shape):
    return jax.ShapeDtypeStruct(shape, jnp.float32)


def on_device(cipher, key_main, key_special, diag_main, diag_special, perms, tw_exp, up_conv, down_conv):
    lead = lax.axis_index("limb")
    main_count = up_conv.shape[0]
    exps = jnp.concatenate(
        [
            lax.dynamic_slice_in_dim(tw_exp, lead * (JS - 1), JS - 1),
            lax.dynamic_slice_in_dim(tw_exp, main_count + lead, 1),
        ]
    )
    tw = twiddle(exps)
    h_a, h_b = jnp.asarray(hartley(A)), jnp.asarray(hartley(B))
    poly = (1, 1, JS - 1, NRING)

    def whole(*shape):
        return pl.BlockSpec(shape, lambda step: (0,) * len(shape))

    coefs = pl.pallas_call(
        inverse_kernel,
        grid=(1,),
        out_shape=f32(LIMBS, (JS - 1) * CHUNK, B),
        in_specs=[
            pl.BlockSpec(poly, lambda step: (0, 1, 0, 0)),
            whole(JS, A, B),
            whole(A, A),
            whole(B, B),
        ],
        out_specs=whole(LIMBS, (JS - 1) * CHUNK, B),
        scratch_shapes=[pltpu.VMEM((JS - 1, A, B), jnp.float32)],
        compiler_params=params(32),
        name="coefficients",
    )(cipher, tw, h_a, h_b)
    columns = exchange(coefs)

    count = lax.axis_size("key")
    ahead = [((target + 1) % count, target) for target in range(count)]
    lanes = NRING // 4
    packed = pl.pallas_call(
        pack_kernel,
        grid=(4,),
        out_shape=jax.ShapeDtypeStruct((32, NRING), jnp.bfloat16),
        in_specs=[
            pl.BlockSpec((1, 2, DNUM, JS - 1, lanes), lambda step: (0, 0, 0, 0, step)),
            pl.BlockSpec((1, 2, DNUM, 1, lanes), lambda step: (0, 0, 0, 0, step)),
            pl.BlockSpec((1, JS - 1, lanes), lambda step: (0, 0, step)),
            pl.BlockSpec((1, 1, lanes), lambda step: (0, 0, step)),
        ],
        out_specs=pl.BlockSpec((32, lanes), lambda step: (0, step)),
        scratch_shapes=[pltpu.VMEM((32, lanes), jnp.float32)],
        compiler_params=params(32),
        name="pack_keys",
    )(key_main, key_special, diag_main, diag_special)
    packed_next = lax.ppermute(packed, "key", ahead)
    perm_own = perms[0]
    perm_next = lax.ppermute(perm_own, "key", ahead)

    raised = pl.pallas_call(
        raise_kernel,
        out_shape=f32(LIMBS, DNUM * JS * CHUNK, B),
        in_specs=[SMEM, VMEM],
        out_specs=VMEM,
        compiler_params=params(32),
        name="raise_digits",
    )(up_conv, columns)
    rise = exchange(raised)

    summed, lowered = pl.pallas_call(
        switch_kernel,
        grid=(1,),
        out_shape=(f32(2 * JS, NRING), f32(LIMBS, 2 * CHUNK, B)),
        in_specs=[
            SMEM,
            SMEM,
            whole(LIMBS, DNUM * JS * CHUNK, B),
            pl.BlockSpec(poly, lambda step: (0, 0, 0, 0)),
            whole(JS, A, B),
            whole(A, A),
            whole(B, B),
            whole(32, NRING),
            whole(32, NRING),
        ],
        out_specs=(whole(2 * JS, NRING), whole(LIMBS, 2 * CHUNK, B)),
        scratch_shapes=[
            pltpu.VMEM((2, A * 16, 128), jnp.float32),
            pltpu.VMEM((NRING, 128), jnp.float32),
            pltpu.VMEM((NRING // 128, 16, 128), jnp.float32),
            pltpu.VMEM((NRING // 128, 16, 128), jnp.float32),
            pltpu.VMEM((2, A, B), jnp.float32),
        ],
        compiler_params=params(56),
        name="switch_keys",
    )(perm_own, perm_next, rise, cipher, tw, h_a, h_b, packed, packed_next)
    special = exchange(lowered)

    returned = pl.pallas_call(
        lower_kernel,
        out_shape=f32(LIMBS, 2 * (JS - 1) * CHUNK, B),
        in_specs=[SMEM, VMEM],
        out_specs=VMEM,
        compiler_params=params(32),
        name="return_limbs",
    )(down_conv, special)
    back = exchange(returned)

    return pl.pallas_call(
        finish_kernel,
        grid=(1,),
        out_shape=f32(1, 2, JS - 1, NRING),
        in_specs=[
            whole(LIMBS, 2 * (JS - 1) * CHUNK, B),
            whole(2 * JS, NRING),
            whole(JS, A, B),
            whole(A, A),
            whole(B, B),
        ],
        out_specs=whole(1, 2, JS - 1, NRING),
        scratch_shapes=[pltpu.VMEM((2, A * 8, 128), jnp.float32)],
        compiler_params=params(32),
        name="finish",
    )(back, summed, tw, h_a, h_b)


def solution(mesh):
    placed = (
        P("key", None, "limb", None),
        P("key", None, None, "limb", None),
        P("key", None, None, "limb", None),
        P("key", "limb", None),
        P("key", "limb", None),
        P("key", None),
        P(),
        P(),
        P(),
    )
    return jax.shard_map(
        on_device,
        mesh=mesh,
        in_specs=placed,
        out_specs=P("key", None, "limb", None),
        check_vma=False,
    )
```

```python
import math

import jax
import jax.numpy as jnp
import numpy as np
from jax import lax
from jax.experimental import pallas as pl
from jax.experimental.pallas import tpu as pltpu
from jax.sharding import PartitionSpec as P

A = 128
B = 256
NRING = A * B
DNUM = 3
LIMBS = 8
JS = 4
CHUNK = A // LIMBS
HIGHEST = lax.Precision.HIGHEST
MIB = 1 << 20
LN2 = math.log(2.0)
LINE = 1024
SLOTS = 4
BLOCKS = 4
ROTS = 2
TAIL = 16
FINE = 16
CODES = 32767.0
STEPS = ((2, 1), (1, 1), (3, 1), (2, 0), (0, 1), (1, 0), (3, 0))

VMEM = pl.BlockSpec(memory_space=pltpu.VMEM)
SMEM = pl.BlockSpec(memory_space=pltpu.SMEM)


def hartley(extent):
    indices = np.arange(extent)
    angles = (indices[:, None] * indices[None, :] % extent) * (2.0 * math.pi / extent)
    return ((np.cos(angles) + np.sin(angles)) / math.sqrt(extent)).astype(np.float32)


def twiddle(exponent):
    product = lax.broadcasted_iota(jnp.int32, (A, B), 0) * lax.broadcasted_iota(jnp.int32, (A, B), 1)
    phase = ((product & (NRING - 1)) * exponent) & (NRING - 1)
    quarter = NRING // 4 - jnp.abs(phase - NRING // 2)
    x = quarter.astype(jnp.float32) * (2.0 * math.pi / NRING)
    y = x * x
    series = 0.0
    for power in (11, 9, 7, 5, 3):
        series = (series + (-1.0) ** (power // 2) / math.factorial(power)) * y
    return 1.0 - 0.5 * (x + x * series)


def params(mib):
    return pltpu.CompilerParams(vmem_limit_bytes=mib * MIB)


def both_sides(h_a, block, h_b):
    half = jnp.dot(h_a, block, precision=HIGHEST, preferred_element_type=jnp.float32)
    return jnp.dot(half, h_b, precision=HIGHEST, preferred_element_type=jnp.float32)


def send_coded(blocks, out_ref):
    top = jnp.max(jnp.abs(blocks[0]))
    for block in blocks[1:]:
        top = jnp.maximum(top, jnp.max(jnp.abs(block)))
    exponent = jnp.ceil(jnp.log(jnp.full((TAIL, B), jnp.maximum(top, 1e-36))) * (FINE / LN2) + 0.125)
    gain = jnp.exp(exponent[:1] * (-LN2 / FINE))
    for at, block in enumerate(blocks):
        root = jnp.sqrt(jnp.sqrt(jnp.abs(block) * gain)) * CODES
        code = jnp.round(jnp.where(block < 0, -root, root)).astype(jnp.int32)
        out_ref[at * A : (at + 1) * A, :] = code.astype(jnp.int16)
    out_ref[len(blocks) * A :, :] = exponent.astype(jnp.int32).astype(jnp.int16)


def received(ref, at):
    tail = ref[ref.shape[0] - TAIL :, :].astype(jnp.int32).astype(jnp.float32)[:1]
    gain = jnp.exp(tail * (LN2 / FINE))
    root = ref[at * A : (at + 1) * A, :].astype(jnp.int32).astype(jnp.float32) * (1.0 / CODES)
    return (root * jnp.abs(root)) * (root * root) * gain


def partner(lead, step, sign):
    z = (lead // 2 + LIMBS + sign * step[0]) % (LIMBS // 2)
    return z * 2 + (lead + step[1]) % 2


def inverse_kernel(lead_ref, exp_ref, cipher_ref, ha_ref, hb_ref, out_ref, x_ref):
    def spread(step, _):
        for limb in range(JS - 1):
            rows = [cipher_ref[0, limb, 1:2, pl.ds(pl.multiple_of((step * 8 + k) * B, B), B)] for k in range(8)]
            x_ref[limb, pl.ds(pl.multiple_of(step * 8, 8), 8), :] = jnp.concatenate(rows, axis=0)
        return 0

    lax.fori_loop(0, A // 8, spread, 0)
    done = []
    for limb in range(JS - 1):
        tw = twiddle(exp_ref[lead_ref[0] * (JS - 1) + limb])
        done.append(both_sides(ha_ref[...], x_ref[limb], hb_ref[...]) / tw)
    send_coded(done, out_ref)


def pack_kernel(km_ref, ks_ref, dm_ref, ds_ref, out_ref, rows_ref):
    for p in range(2):
        for digit in range(DNUM):
            at = p * 16 + digit * JS
            rows_ref[at : at + JS - 1, :] = km_ref[0, p, digit].astype(jnp.float32)
            rows_ref[at + JS - 1 : at + JS, :] = ks_ref[0, p, digit].astype(jnp.float32)
        at = p * 16 + DNUM * JS
        rows_ref[at : at + JS - 1, :] = dm_ref[0].astype(jnp.float32)
        rows_ref[at + JS - 1 : at + JS, :] = ds_ref[0].astype(jnp.float32)
    out_ref[...] = rows_ref[...].astype(jnp.bfloat16)


def gather_kernel(
    lead_ref, exp_ref, up_ref, idx_ref, base_ref, ha_ref, hb_ref, own_ref, *rest,
):
    arrived, (got_ref, coef_ref, raised_ref, rows_ref, ext_ref, *slots, arrive) = rest[: len(STEPS)], rest[len(STEPS) :]
    chunks = ROTS * NRING // LINE

    def fetch(chunk, slot):
        place = pl.ds(pl.multiple_of(chunk * LINE, LINE), LINE)
        return pltpu.make_async_copy(idx_ref.at[place], slots[slot], arrive.at[slot])

    for slot in range(SLOTS):
        fetch(slot, slot).start()
    lead = lead_ref[0]
    for step, ref in zip(((0, 0),) + STEPS, (own_ref,) + arrived):
        source = partner(lead, step, -1)
        for limb in range(JS - 1):
            coef_ref[source * (JS - 1) + limb] = received(ref, limb)

    def lift(step, _):
        rows = pl.ds(pl.multiple_of(step * CHUNK, CHUNK), CHUNK)
        for digit in range(DNUM):
            limbs = range(digit * LIMBS, (digit + 1) * LIMBS)
            parts = [coef_ref[limb, rows, :] for limb in limbs]
            for j in range(JS):
                m = lead * (JS - 1) + j if j < JS - 1 else LIMBS * (JS - 1) + lead
                total = None
                for limb, part in zip(limbs, parts):
                    term = up_ref[limb, m] * part
                    total = term if total is None else total + term
                raised_ref[digit * JS + j, rows, :] = total
        return 0

    lax.fori_loop(0, LIMBS, lift, 0)

    for j in range(JS):
        tw = twiddle(exp_ref[lead * (JS - 1) + j if j < JS - 1 else LIMBS * (JS - 1) + lead])
        for digit in range(DNUM):
            ch = digit * JS + j
            done = both_sides(ha_ref[...], raised_ref[ch] * tw, hb_ref[...])
            rows_ref[0, pl.ds(ch, A, stride=16), :] = done[:, :128]
            rows_ref[1, pl.ds(ch, A, stride=16), :] = done[:, 128:]

    def first(i, _):
        for half in range(2):
            lanes = pl.ds(pl.multiple_of(i * B + half * 128, 128), 128)
            lines = [base_ref[0, limb, 0:1, lanes] for limb in range(JS - 1)] + [jnp.zeros((1, 128), jnp.float32)]
            rows_ref[half, pl.ds(pl.multiple_of(i * 16 + 8, 8) + 4, 4), :] = jnp.concatenate(lines, axis=0)
        return 0

    lax.fori_loop(0, A, first, 0)

    def turn(step, _):
        for k in range(4):
            i = step * 4 + k
            for half in range(2):
                part = rows_ref[half, pl.ds(pl.multiple_of(i * 16, 16), 16), :]
                ext_ref[pl.ds(pl.multiple_of(i * B + half * 128, 128), 128), :] = jnp.concatenate([part] * 8, axis=0).T
        return 0

    lax.fori_loop(0, A // 4, turn, 0)

    group = lax.broadcasted_iota(jnp.int32, (1, 128), 1) // 16

    def gather(step, _):
        for slot in range(SLOTS):
            chunk = step * SLOTS + slot
            fetch(chunk, slot).wait()
            for r in range(128):
                row = None
                for g in range(8):
                    one = ext_ref[pl.ds(slots[slot][g * 128 + r], 1), :]
                    row = one if row is None else jnp.where(group == g, one, row)
                got_ref[chunk, r : r + 1, :] = row

            @pl.when(step < chunks // SLOTS - 1)
            def _():
                fetch(chunk + SLOTS, slot).start()

        return 0

    lax.fori_loop(0, chunks // SLOTS, gather, 0)


def combine_kernel(
    lead_ref, exp_ref, got0_ref, got1_ref, ha_ref, hb_ref, k0_ref, k1_ref, sum_ref, low_ref, spec_ref,
):
    sub = lax.broadcasted_iota(jnp.int32, (8, 128), 0)
    low_half = sub < JS
    base_gain = jnp.where((sub >= JS) & (sub < 2 * JS - 1), 1.0, 0.0).astype(jnp.float32)
    step = pl.program_id(0)
    for part in range(BLOCKS // 2):
        lines = [[[], []], [[], []]]
        for k in range(16):
            blk, g = part * 2 + k // 8, k % 8
            if g == 0:
                turned = [ref[blk].T for ref in (got0_ref, got1_ref)]
            lanes = slice(blk * LINE + g * 128, blk * LINE + g * 128 + 128)
            sums = [None, None]
            for s, k_ref in enumerate((k0_ref, k1_ref)):
                keys = k_ref[:, lanes].astype(jnp.float32)
                upper = turned[s][g * 16 : g * 16 + 8]
                lower = turned[s][g * 16 + 8 : g * 16 + 16]
                tail = keys[8:16]
                diag = jnp.where(low_half, jnp.roll(tail, JS, axis=0), tail)
                for p in range(2):
                    gain = jnp.where(low_half, keys[p * 16 + 8 : p * 16 + 16], base_gain if p == 0 else 0.0)
                    term = diag * (keys[p * 16 : p * 16 + 8] * upper + gain * lower)
                    sums[p] = term if sums[p] is None else sums[p] + term
            folded = [value + jnp.roll(value, JS, axis=0) for value in sums]
            both = jnp.where(low_half, folded[0], folded[1])
            sum_ref[:, lanes] = both
            for p in range(2):
                lines[p][k % 2].append(both[p * JS + JS - 1 : p * JS + JS])
        at = pl.ds(pl.multiple_of(step * (BLOCKS * 4) + part * 8, 8), 8)
        for p in range(2):
            for half in range(2):
                spec_ref[p, at, half * 128 : (half + 1) * 128] = jnp.concatenate(lines[p][half], axis=0)

    @pl.when(step == pl.num_programs(0) - 1)
    def _():
        tw = twiddle(exp_ref[LIMBS * (JS - 1) + lead_ref[0]])
        send_coded([both_sides(ha_ref[...], spec_ref[p], hb_ref[...]) / tw for p in range(2)], low_ref)


def finish_kernel(lead_ref, exp_ref, down_ref, sum_ref, ha_ref, hb_ref, own_ref, *rest):
    arrived, (out_ref, low_ref, returned_ref, rows_ref) = rest[: len(STEPS)], rest[len(STEPS) :]
    lead = lead_ref[0]
    for step, ref in zip(((0, 0),) + STEPS, (own_ref,) + arrived):
        source = partner(lead, step, -1)
        for p in range(2):
            low_ref[source * 2 + p] = received(ref, p)

    def lower(step, _):
        rows = pl.ds(pl.multiple_of(step * CHUNK, CHUNK), CHUNK)
        for p in range(2):
            parts = [low_ref[k * 2 + p, rows, :] for k in range(LIMBS)]
            for j in range(JS - 1):
                total = None
                for k, part in enumerate(parts):
                    term = down_ref[k, lead * (JS - 1) + j] * part
                    total = term if total is None else total + term
                returned_ref[p * (JS - 1) + j, rows, :] = total
        return 0

    lax.fori_loop(0, LIMBS, lower, 0)
    for j in range(JS - 1):
        tw = twiddle(exp_ref[lead * (JS - 1) + j])
        for p in range(2):
            done = both_sides(ha_ref[...], returned_ref[p * (JS - 1) + j] * tw, hb_ref[...])
            rows_ref[0, pl.ds(p * JS + j, A, stride=8), :] = done[:, :128]
            rows_ref[1, pl.ds(p * JS + j, A, stride=8), :] = done[:, 128:]

    def body(i, _):
        for half in range(2):
            lanes = pl.ds(pl.multiple_of(i * B + half * 128, 128), 128)
            left = sum_ref[:, lanes] - rows_ref[half, pl.ds(pl.multiple_of(i * 8, 8), 8), :]
            for j in range(JS - 1):
                out_ref[0, j, :, lanes] = jnp.concatenate([left[j : j + 1], left[JS + j : JS + j + 1]], axis=0)
        return 0

    lax.fori_loop(0, A, body, 0)


def spread_limbs(value):
    return [value] + [
        lax.ppermute(value, "limb", [(source, partner(source, step, 1)) for source in range(LIMBS)])
        for step in STEPS
    ]


def f32(*shape):
    return jax.ShapeDtypeStruct(shape, jnp.float32)


def cost(micros):
    return pl.CostEstimate(flops=int(micros * 1e9), bytes_accessed=1 << 20, transcendentals=0)


def on_device(cipher, key_main, key_special, diag_main, diag_special, perms, tw_exp, up_conv, down_conv):
    lead = lax.axis_index("limb").astype(jnp.int32)[None]
    h_a, h_b = jnp.asarray(hartley(A)), jnp.asarray(hartley(B))
    cipher = cipher.transpose(0, 2, 1, 3)

    coefs = pl.pallas_call(
        inverse_kernel,
        out_shape=jax.ShapeDtypeStruct(((JS - 1) * A + TAIL, B), jnp.int16),
        in_specs=[SMEM, SMEM, VMEM, VMEM, VMEM],
        out_specs=VMEM,
        scratch_shapes=[pltpu.VMEM((JS - 1, A, B), jnp.float32)],
        compiler_params=params(32),
        cost_estimate=cost(2),
        name="coefficients",
    )(lead, tw_exp, cipher, h_a, h_b)
    held = spread_limbs(coefs)

    count = lax.axis_size("key")
    ahead = [((target + 1) % count, target) for target in range(count)]
    key_main, key_special, diag_main, diag_special, perm_own, _ = lax.optimization_barrier(
        (key_main, key_special, diag_main, diag_special, perms[0], coefs)
    )
    both_perms = jnp.concatenate([perm_own, lax.ppermute(perm_own, "key", ahead)])
    lanes = NRING // 4
    packed = pl.pallas_call(
        pack_kernel,
        grid=(4,),
        out_shape=jax.ShapeDtypeStruct((32, NRING), jnp.bfloat16),
        in_specs=[
            pl.BlockSpec((1, 2, DNUM, JS - 1, lanes), lambda step: (0, 0, 0, 0, step)),
            pl.BlockSpec((1, 2, DNUM, 1, lanes), lambda step: (0, 0, 0, 0, step)),
            pl.BlockSpec((1, JS - 1, lanes), lambda step: (0, 0, step)),
            pl.BlockSpec((1, 1, lanes), lambda step: (0, 0, step)),
        ],
        out_specs=pl.BlockSpec((32, lanes), lambda step: (0, step)),
        scratch_shapes=[pltpu.VMEM((32, lanes), jnp.float32)],
        compiler_params=params(32),
        cost_estimate=cost(2),
        name="pack_keys",
    )(key_main, key_special, diag_main, diag_special)
    packed, both_perms, *held = lax.optimization_barrier((packed, both_perms, *held))
    packed_next = lax.ppermute(packed, "key", ahead)

    gathered = pl.pallas_call(
        gather_kernel,
        out_shape=f32(ROTS * NRING // LINE, 128, 128),
        in_specs=[SMEM] * 3 + [pl.BlockSpec(memory_space=pl.ANY)] + [VMEM] * (4 + len(STEPS)),
        out_specs=VMEM,
        scratch_shapes=[
            pltpu.VMEM((LIMBS * (JS - 1), A, B), jnp.float32),
            pltpu.VMEM((DNUM * JS, A, B), jnp.float32),
            pltpu.VMEM((2, A * 16, 128), jnp.float32),
            pltpu.VMEM((NRING, 128), jnp.float32),
        ]
        + [pltpu.SMEM((LINE,), jnp.int32)] * SLOTS
        + [pltpu.SemaphoreType.DMA((SLOTS,))],
        compiler_params=params(56),
        cost_estimate=cost(50),
        name="extend_and_gather",
    )(lead, tw_exp, up_conv, both_perms, cipher, h_a, h_b, *held)

    steps = NRING // LINE // BLOCKS
    lines = (BLOCKS, 128, 128)
    keys = pl.BlockSpec((32, BLOCKS * LINE), lambda step: (0, step))
    low_shape = (2 * A + TAIL, B)
    summed, lowered = pl.pallas_call(
        combine_kernel,
        grid=(steps,),
        out_shape=(f32(2 * JS, NRING), jax.ShapeDtypeStruct(low_shape, jnp.int16)),
        in_specs=[SMEM] * 2
        + [
            pl.BlockSpec(lines, lambda step: (step, 0, 0)),
            pl.BlockSpec(lines, lambda step: (step + steps, 0, 0)),
            pl.BlockSpec((A, A), lambda step: (0, 0)),
            pl.BlockSpec((B, B), lambda step: (0, 0)),
            keys,
            keys,
        ],
        out_specs=(
            pl.BlockSpec((2 * JS, BLOCKS * LINE), lambda step: (0, step)),
            pl.BlockSpec(low_shape, lambda step: (0, 0)),
        ),
        scratch_shapes=[pltpu.VMEM((2, A, B), jnp.float32)],
        compiler_params=params(32),
        cost_estimate=cost(5),
        name="switch_keys",
    )(lead, tw_exp, gathered, gathered, h_a, h_b, packed, packed_next)
    special = spread_limbs(lowered)

    result = pl.pallas_call(
        finish_kernel,
        out_shape=f32(1, JS - 1, 2, NRING),
        in_specs=[SMEM] * 3 + [VMEM] * (4 + len(STEPS)),
        out_specs=VMEM,
        scratch_shapes=[
            pltpu.VMEM((LIMBS * 2, A, B), jnp.float32),
            pltpu.VMEM((2 * (JS - 1), A, B), jnp.float32),
            pltpu.VMEM((2, A * 8, 128), jnp.float32),
        ],
        compiler_params=params(32),
        cost_estimate=cost(4),
        name="finish",
    )(lead, tw_exp, down_conv, summed, h_a, h_b, *special)
    return result.transpose(0, 2, 1, 3)


def solution(mesh):
    placed = (
        P("key", None, "limb", None),
        P("key", None, None, "limb", None),
        P("key", None, None, "limb", None),
        P("key", "limb", None),
        P("key", "limb", None),
        P("key", None),
        P(),
        P(),
        P(),
    )
    return jax.shard_map(
        on_device,
        mesh=mesh,
        in_specs=placed,
        out_specs=P("key", None, "limb", None),
        check_vma=False,
    )
```

```python
import functools
import math

import jax
import jax.numpy as jnp
import numpy as np
from jax import lax
from jax.experimental import pallas as pl
from jax.experimental.pallas import tpu as pltpu
from jax.sharding import PartitionSpec as P

A = 128
B = 256
NRING = A * B
DNUM = 3
LIMBS = 8
JS = 4
CHUNK = A // LIMBS
HIGHEST = lax.Precision.HIGHEST
MIB = 1 << 20
LN2 = math.log(2.0)
LINE = 1024
SLOTS = 4
CHIPS_Z = 4
BLOCKS = 4
ROTS = 2
TAIL = 16
FINE = 16
CODES = 32767.0

VMEM = pl.BlockSpec(memory_space=pltpu.VMEM)
SMEM = pl.BlockSpec(memory_space=pltpu.SMEM)


def hartley(extent):
    indices = np.arange(extent)
    angles = (indices[:, None] * indices[None, :] % extent) * (2.0 * math.pi / extent)
    return ((np.cos(angles) + np.sin(angles)) / math.sqrt(extent)).astype(np.float32)


def twiddle(exponent):
    product = lax.broadcasted_iota(jnp.int32, (A, B), 0) * lax.broadcasted_iota(jnp.int32, (A, B), 1)
    phase = ((product & (NRING - 1)) * exponent) & (NRING - 1)
    quarter = NRING // 4 - jnp.abs(phase - NRING // 2)
    x = quarter.astype(jnp.float32) * (2.0 * math.pi / NRING)
    y = x * x
    series = 0.0
    for power in (11, 9, 7, 5, 3):
        series = (series + (-1.0) ** (power // 2) / math.factorial(power)) * y
    return 1.0 - 0.5 * (x + x * series)


def params(mib):
    return pltpu.CompilerParams(vmem_limit_bytes=mib * MIB)


def parts(value):
    high = value.astype(jnp.bfloat16)
    return high, (value - high.astype(jnp.float32)).astype(jnp.bfloat16)


def product(left, right):
    terms = [(left[0], right[0]), (left[0], right[1]), (left[1], right[0])]
    done = [jnp.dot(x, y, preferred_element_type=jnp.float32) for x, y in terms]
    return done[0] + (done[1] + done[2])


def both_sides(h_a, block, h_b):
    return product(parts(product(h_a, parts(block))), h_b)


def send_coded(blocks, out_ref, copies):
    top = jnp.max(jnp.abs(blocks[0]))
    for block in blocks[1:]:
        top = jnp.maximum(top, jnp.max(jnp.abs(block)))
    exponent = jnp.ceil(jnp.log(jnp.full((TAIL, B), jnp.maximum(top, 1e-36))) * (FINE / LN2) + 0.125)
    gain = jnp.exp(exponent[:1] * (-LN2 / FINE))
    for at, block in enumerate(blocks):
        root = jnp.sqrt(jnp.sqrt(jnp.abs(block) * gain)) * CODES
        code = jnp.round(jnp.where(block < 0, -root, root)).astype(jnp.int32).astype(jnp.int16)
        for to in range(copies):
            out_ref[to, at * A : (at + 1) * A, :] = code
    scale = exponent.astype(jnp.int32).astype(jnp.int16)
    for to in range(copies):
        out_ref[to, len(blocks) * A :, :] = scale


def received(ref, source, at):
    rows = ref.shape[1]
    tail = ref[source, rows - TAIL : rows, :].astype(jnp.int32).astype(jnp.float32)[:1]
    gain = jnp.exp(tail * (LN2 / FINE))
    root = ref[source, at * A : (at + 1) * A, :].astype(jnp.int32).astype(jnp.float32) * (1.0 / CODES)
    return (root * jnp.abs(root)) * (root * root) * gain


def inverse_kernel(lead_ref, exp_ref, cipher_ref, ha_ref, hb_ref, out_ref, x_ref):
    def spread(step, _):
        for limb in range(JS - 1):
            rows = [cipher_ref[0, limb, 1:2, pl.ds(pl.multiple_of((step * 8 + k) * B, B), B)] for k in range(8)]
            x_ref[limb, pl.ds(pl.multiple_of(step * 8, 8), 8), :] = jnp.concatenate(rows, axis=0)
        return 0

    lax.fori_loop(0, A // 8, spread, 0)
    h_a, h_b = parts(ha_ref[...]), parts(hb_ref[...])
    done = []
    for limb in range(JS - 1):
        tw = twiddle(exp_ref[lead_ref[0] * (JS - 1) + limb])
        done.append(both_sides(h_a, x_ref[limb], h_b) / tw)
    send_coded(done, out_ref, 1)


def pack_kernel(km_ref, ks_ref, dm_ref, ds_ref, out_ref, rows_ref):
    for p in range(2):
        for digit in range(DNUM):
            at = p * 16 + digit * JS
            rows_ref[at : at + JS - 1, :] = km_ref[0, p, digit].astype(jnp.float32)
            rows_ref[at + JS - 1 : at + JS, :] = ks_ref[0, p, digit].astype(jnp.float32)
        at = p * 16 + DNUM * JS
        rows_ref[at : at + JS - 1, :] = dm_ref[0].astype(jnp.float32)
        rows_ref[at + JS - 1 : at + JS, :] = ds_ref[0].astype(jnp.float32)
    out_ref[...] = rows_ref[...].astype(jnp.bfloat16)


def combine(block, keys_ref, lanes_of, before_ref, sum_ref):
    sub = lax.broadcasted_iota(jnp.int32, (8, 128), 0)
    low_half = sub < JS
    base_gain = jnp.where((sub >= JS) & (sub < 2 * JS - 1), 1.0, 0.0).astype(jnp.float32)
    special = [[[], []], [[], []]]
    turned = block.T
    for g in range(8):
        lanes = lanes_of(g)
        keys = keys_ref[:, lanes].astype(jnp.float32)
        upper = turned[g * 16 : g * 16 + 8]
        lower = turned[g * 16 + 8 : g * 16 + 16]
        tail = keys[8:16]
        diag = jnp.where(low_half, jnp.roll(tail, JS, axis=0), tail)
        folded = []
        for p in range(2):
            gain = jnp.where(low_half, keys[p * 16 + 8 : p * 16 + 16], base_gain if p == 0 else 0.0)
            term = diag * (keys[p * 16 : p * 16 + 8] * upper + gain * lower)
            folded.append(term + jnp.roll(term, JS, axis=0))
        both = jnp.where(low_half, folded[0], folded[1])
        if before_ref is not None:
            both = both + before_ref[:, lanes]
        sum_ref[:, lanes] = both
        for p in range(2):
            special[p][g % 2].append(both[p * JS + JS - 1 : p * JS + JS])
    return special


def extend_kernel(
    lead_ref, exp_ref, up_ref, idx_ref, base_ref, ha_ref, hb_ref, keys_ref, held0_ref, held1_ref, held2_ref, held3_ref,
    sum_ref, got_ref, coef_ref, raised_ref, rows_ref, turns_ref, ext_ref, *rest,
):
    slots, got, arrive = rest[:SLOTS], rest[SLOTS : 2 * SLOTS], rest[-1]
    chunks = ROTS * NRING // LINE

    def fetch(chunk, slot):
        place = pl.ds(pl.multiple_of(chunk * LINE, LINE), LINE)
        return pltpu.make_async_copy(idx_ref.at[place], slots[slot], arrive.at[slot])

    for slot in range(SLOTS):
        fetch(slot, slot).start()
    lead = lead_ref[0]
    for step, held_ref in enumerate((held0_ref, held1_ref, held2_ref, held3_ref)):
        for across in range(2):
            source = (lead // 2 + CHIPS_Z - step) % CHIPS_Z * 2 + (lead + across) % 2
            for limb in range(JS - 1):
                coef_ref[source * (JS - 1) + limb] = received(held_ref, across, limb)

    def lift(step, _):
        rows = pl.ds(pl.multiple_of(step * CHUNK, CHUNK), CHUNK)
        for digit in range(DNUM):
            limbs = range(digit * LIMBS, (digit + 1) * LIMBS)
            parts = [coef_ref[limb, rows, :] for limb in limbs]
            for j in range(JS):
                m = lead * (JS - 1) + j if j < JS - 1 else LIMBS * (JS - 1) + lead
                total = None
                for limb, part in zip(limbs, parts):
                    term = up_ref[limb, m] * part
                    total = term if total is None else total + term
                raised_ref[digit * JS + j, rows, :] = total
        return 0

    lax.fori_loop(0, LIMBS, lift, 0)

    h_a, h_b = parts(ha_ref[...]), parts(hb_ref[...])
    for j in range(JS):
        tw = twiddle(exp_ref[lead * (JS - 1) + j if j < JS - 1 else LIMBS * (JS - 1) + lead])
        for digit in range(DNUM):
            ch = digit * JS + j
            done = both_sides(h_a, raised_ref[ch] * tw, h_b)
            rows_ref[0, pl.ds(ch, A, stride=16), :] = done[:, :128]
            rows_ref[1, pl.ds(ch, A, stride=16), :] = done[:, 128:]

    def first(i, _):
        for half in range(2):
            lanes = pl.ds(pl.multiple_of(i * B + half * 128, 128), 128)
            lines = [base_ref[0, limb, 0:1, lanes] for limb in range(JS - 1)] + [jnp.zeros((1, 128), jnp.float32)]
            rows_ref[half, pl.ds(pl.multiple_of(i * 16 + 8, 8) + 4, 4), :] = jnp.concatenate(lines, axis=0)
        return 0

    lax.fori_loop(0, A, first, 0)

    source = lax.broadcasted_iota(jnp.int32, (2 * 128, 128), 0) & 127
    target = lax.broadcasted_iota(jnp.int32, (2 * 128, 128), 1)
    for by in range(8):
        ones = jnp.where(((source + by * 16) & 127) == target, 1.0, 0.0)
        turns_ref[:, by * 128 : (by + 1) * 128] = ones.astype(jnp.bfloat16)

    def turn(step, _):
        for half in range(2):
            block = rows_ref[half, pl.ds(pl.multiple_of(step * 128, 128), 128), :].T
            both = jnp.concatenate(parts(block), axis=1)
            turned = jnp.dot(both, turns_ref[...], preferred_element_type=jnp.float32)
            for by in range(8):
                at = pl.ds(pl.multiple_of(by * (NRING // 8) + step * B + half * 128, 128), 128)
                ext_ref[at, :] = turned[:, by * 128 : (by + 1) * 128]
        return 0

    lax.fori_loop(0, A // 8, turn, 0)


    group = lax.broadcasted_iota(jnp.int32, (1, 128), 1) // 16

    def gather(chunk, slot, store):
        fetch(chunk, slot).wait()
        for r in range(128):
            row = None
            for g in range(8):
                one = ext_ref[pl.ds(slots[slot][g * 128 + r], 1), :]
                row = one if row is None else jnp.where(group == g, one, row)
            store(r, row)

    def own(step, _):
        def product_of(chunk, slot):
            lanes_of = lambda g: pl.ds(pl.multiple_of(chunk * LINE + g * 128, 128), 128)
            combine(got[slot][...], keys_ref, lanes_of, None, sum_ref)

        for slot in range(SLOTS):
            chunk = step * SLOTS + slot

            def store(r, row, slot=slot):
                got[slot][r : r + 1, :] = row

            gather(chunk, slot, store)
            if slot > 0:
                product_of(chunk - 1, slot - 1)
            fetch(chunk + SLOTS, slot).start()
        product_of(step * SLOTS + SLOTS - 1, SLOTS - 1)
        return 0

    lax.fori_loop(0, chunks // 2 // SLOTS, own, 0)

    def other(step, _):
        for slot in range(SLOTS):
            chunk = step * SLOTS + slot

            def store(r, row, chunk=chunk):
                got_ref[chunk - chunks // 2, r : r + 1, :] = row

            gather(chunk, slot, store)
            fetch(jnp.minimum(chunk + SLOTS, chunks - 1), slot).start()
        return 0

    lax.fori_loop(chunks // 2 // SLOTS, chunks // SLOTS, other, 0)
    for slot in range(SLOTS):
        fetch(chunks - 1, slot).wait()


def combine_kernel(
    lead_ref, exp_ref, got_ref, ha_ref, hb_ref, keys_ref, before_ref, sum_ref, low_ref, spec_ref,
):
    step = pl.program_id(0)
    for pair in range(BLOCKS // 2):
        done = []
        for blk in (2 * pair, 2 * pair + 1):
            lanes_of = lambda g: slice(blk * LINE + g * 128, blk * LINE + g * 128 + 128)
            done.append(combine(got_ref[blk], keys_ref, lanes_of, before_ref, sum_ref))
        at = pl.ds(pl.multiple_of(step * (BLOCKS * 4) + pair * 8, 8), 8)
        for p in range(2):
            for half in range(2):
                eight = done[0][p][half] + done[1][p][half]
                spec_ref[p, at, half * 128 : (half + 1) * 128] = jnp.concatenate(eight, axis=0)

    @pl.when(step == pl.num_programs(0) - 1)
    def _():
        tw = twiddle(exp_ref[LIMBS * (JS - 1) + lead_ref[0]])
        h_a, h_b = parts(ha_ref[...]), parts(hb_ref[...])
        send_coded([both_sides(h_a, spec_ref[p], h_b) / tw for p in range(2)], low_ref, LIMBS)


def finish_kernel(lead_ref, exp_ref, down_ref, sum_ref, ha_ref, hb_ref, held_ref, out_ref, low_ref, returned_ref, rows_ref):
    lead = lead_ref[0]
    h_a, h_b = parts(ha_ref[...]), parts(hb_ref[...])
    for source in range(LIMBS):
        for p in range(2):
            low_ref[source * 2 + p] = received(held_ref, source, p)

    def lower(step, _):
        rows = pl.ds(pl.multiple_of(step * CHUNK, CHUNK), CHUNK)
        for p in range(2):
            parts = [low_ref[k * 2 + p, rows, :] for k in range(LIMBS)]
            for j in range(JS - 1):
                total = None
                for k, part in enumerate(parts):
                    term = down_ref[k, lead * (JS - 1) + j] * part
                    total = term if total is None else total + term
                returned_ref[p * (JS - 1) + j, rows, :] = total
        return 0

    lax.fori_loop(0, LIMBS, lower, 0)
    for j in range(JS - 1):
        tw = twiddle(exp_ref[lead * (JS - 1) + j])
        for p in range(2):
            done = both_sides(h_a, returned_ref[p * (JS - 1) + j] * tw, h_b)
            rows_ref[0, pl.ds(p * JS + j, A, stride=8), :] = done[:, :128]
            rows_ref[1, pl.ds(p * JS + j, A, stride=8), :] = done[:, 128:]

    def body(i, _):
        for half in range(2):
            lanes = pl.ds(pl.multiple_of(i * B + half * 128, 128), 128)
            left = sum_ref[:, lanes] - rows_ref[half, pl.ds(pl.multiple_of(i * 8, 8), 8), :]
            for j in range(JS - 1):
                out_ref[0, j, :, lanes] = jnp.concatenate([left[j : j + 1], left[JS + j : JS + j + 1]], axis=0)
        return 0

    lax.fori_loop(0, A, body, 0)


def exchange(value):
    return lax.all_to_all(value, "limb", split_axis=0, concat_axis=0, tiled=True)


def rows_of(perms):
    place = jnp.arange(perms.shape[0], dtype=jnp.int32) >> 7
    by = (place - (perms >> 8)) & 7
    return (by << 12) + ((perms >> 11) << 8) + (perms & (B - 1))


def f32(*shape):
    return jax.ShapeDtypeStruct(shape, jnp.float32)


def cost(micros):
    return pl.CostEstimate(flops=int(micros * 1e9), bytes_accessed=1 << 20, transcendentals=0)


def on_device(cipher, key_main, key_special, diag_main, diag_special, perms, tw_exp, up_conv, down_conv):
    lead = lax.axis_index("limb").astype(jnp.int32)[None]
    h_a, h_b = jnp.asarray(hartley(A)), jnp.asarray(hartley(B))
    cipher = cipher.transpose(0, 2, 1, 3)

    coefs = pl.pallas_call(
        inverse_kernel,
        out_shape=jax.ShapeDtypeStruct((1, (JS - 1) * A + TAIL, B), jnp.int16),
        in_specs=[SMEM, SMEM, VMEM, VMEM, VMEM],
        out_specs=VMEM,
        scratch_shapes=[pltpu.VMEM((JS - 1, A, B), jnp.float32)],
        compiler_params=params(60),
        cost_estimate=cost(2),
        name="coefficients",
    )(lead, tw_exp, cipher, h_a, h_b)
    pair = jnp.concatenate([coefs, lax.ppermute(coefs, "limb", [(source, source ^ 1) for source in range(LIMBS)])])
    held = [pair] + [
        lax.ppermute(pair, "limb", [(source, (source + 2 * step) % LIMBS) for source in range(LIMBS)])
        for step in range(1, CHIPS_Z)
    ]

    count = lax.axis_size("key")
    ahead = [((target + 1) % count, target) for target in range(count)]
    key_main, key_special, diag_main, diag_special, _ = lax.optimization_barrier(
        (key_main, key_special, diag_main, diag_special, coefs)
    )
    lanes = NRING // 4
    packed = pl.pallas_call(
        pack_kernel,
        grid=(4,),
        out_shape=jax.ShapeDtypeStruct((32, NRING), jnp.bfloat16),
        in_specs=[
            pl.BlockSpec((1, 2, DNUM, JS - 1, lanes), lambda step: (0, 0, 0, 0, step)),
            pl.BlockSpec((1, 2, DNUM, 1, lanes), lambda step: (0, 0, 0, 0, step)),
            pl.BlockSpec((1, JS - 1, lanes), lambda step: (0, 0, step)),
            pl.BlockSpec((1, 1, lanes), lambda step: (0, 0, step)),
        ],
        out_specs=pl.BlockSpec((32, lanes), lambda step: (0, step)),
        scratch_shapes=[pltpu.VMEM((32, lanes), jnp.float32)],
        compiler_params=params(32),
        cost_estimate=cost(2),
        name="pack_keys",
    )(key_main, key_special, diag_main, diag_special)
    perm_own, packed = lax.optimization_barrier((perms[0], packed))
    both_rows = rows_of(jnp.concatenate([perm_own, lax.ppermute(perm_own, "key", ahead)]))
    packed, both_rows, *held = lax.optimization_barrier((packed, both_rows, *held))
    packed_next = lax.ppermute(packed, "key", ahead)

    half_lines = NRING // LINE
    first, gathered = pl.pallas_call(
        extend_kernel,
        out_shape=(f32(2 * JS, NRING), f32(half_lines, 128, 128)),
        in_specs=[SMEM] * 3 + [pl.BlockSpec(memory_space=pl.ANY)] + [VMEM] * 8,
        out_specs=(VMEM, VMEM),
        scratch_shapes=[
            pltpu.VMEM((LIMBS * (JS - 1), A, B), jnp.float32),
            pltpu.VMEM((DNUM * JS, A, B), jnp.float32),
            pltpu.VMEM((2, A * 16, 128), jnp.float32),
            pltpu.VMEM((2 * 128, 8 * 128), jnp.bfloat16),
            pltpu.VMEM((NRING, 128), jnp.float32),
        ]
        + [pltpu.SMEM((LINE,), jnp.int32)] * SLOTS
        + [pltpu.VMEM((128, 128), jnp.float32)] * SLOTS
        + [pltpu.SemaphoreType.DMA((SLOTS,))],
        compiler_params=params(40),
        cost_estimate=cost(50),
        name="extend_and_gather",
    )(lead, tw_exp, up_conv, both_rows, cipher, h_a, h_b, packed, *held)

    lines = (BLOCKS, 128, 128)
    columns = pl.BlockSpec((2 * JS, BLOCKS * LINE), lambda step: (0, step))
    low_shape = (LIMBS, 2 * A + TAIL, B)
    summed, lowered = pl.pallas_call(
        combine_kernel,
        grid=(half_lines // BLOCKS,),
        out_shape=(f32(2 * JS, NRING), jax.ShapeDtypeStruct(low_shape, jnp.int16)),
        in_specs=[SMEM] * 2
        + [
            pl.BlockSpec(lines, lambda step: (step, 0, 0)),
            pl.BlockSpec((A, A), lambda step: (0, 0)),
            pl.BlockSpec((B, B), lambda step: (0, 0)),
            pl.BlockSpec((32, BLOCKS * LINE), lambda step: (0, step)),
            columns,
        ],
        out_specs=(columns, pl.BlockSpec(low_shape, lambda step: (0, 0, 0))),
        scratch_shapes=[pltpu.VMEM((2, A, B), jnp.float32)],
        compiler_params=params(32),
        cost_estimate=cost(4),
        name="switch_next",
    )(lead, tw_exp, gathered, h_a, h_b, packed_next, first)
    special = exchange(lowered)

    result = pl.pallas_call(
        finish_kernel,
        out_shape=f32(1, JS - 1, 2, NRING),
        in_specs=[SMEM] * 3 + [VMEM] * 4,
        out_specs=VMEM,
        scratch_shapes=[
            pltpu.VMEM((LIMBS * 2, A, B), jnp.float32),
            pltpu.VMEM((2 * (JS - 1), A, B), jnp.float32),
            pltpu.VMEM((2, A * 8, 128), jnp.float32),
        ],
        compiler_params=params(60),
        cost_estimate=cost(4),
        name="finish",
    )(lead, tw_exp, down_conv, summed, h_a, h_b, special)
    return result.transpose(0, 2, 1, 3)


def solution(mesh):
    placed = (
        P("key", None, "limb", None),
        P("key", None, None, "limb", None),
        P("key", None, None, "limb", None),
        P("key", "limb", None),
        P("key", "limb", None),
        P("key", None),
        P(),
        P(),
        P(),
    )
    return jax.shard_map(
        on_device,
        mesh=mesh,
        in_specs=placed,
        out_specs=P("key", None, "limb", None),
        check_vma=False,
    )
```

```python
import functools
import math

import jax
import jax.numpy as jnp
import numpy as np
from jax import lax
from jax.experimental import pallas as pl
from jax.experimental.pallas import tpu as pltpu
from jax.sharding import PartitionSpec as P

A = 128
B = 256
NRING = A * B
DNUM = 3
LIMBS = 8
JS = 4
CHUNK = A // LIMBS
HIGHEST = lax.Precision.HIGHEST
MIB = 1 << 20
LN2 = math.log(2.0)
LINE = 1024
SLOTS = 4
STEPS = ((0, 0), (3, 0), (1, 0), (0, 1), (2, 0), (3, 1), (1, 1), (2, 1))
BLOCKS = 4
ROTS = 2
TAIL = 16
FINE = 16
CODES = 32767.0

VMEM = pl.BlockSpec(memory_space=pltpu.VMEM)
SMEM = pl.BlockSpec(memory_space=pltpu.SMEM)


def hartley(extent):
    indices = np.arange(extent)
    angles = (indices[:, None] * indices[None, :] % extent) * (2.0 * math.pi / extent)
    return ((np.cos(angles) + np.sin(angles)) / math.sqrt(extent)).astype(np.float32)


def twiddle(exponent):
    product = lax.broadcasted_iota(jnp.int32, (A, B), 0) * lax.broadcasted_iota(jnp.int32, (A, B), 1)
    phase = ((product & (NRING - 1)) * exponent) & (NRING - 1)
    quarter = NRING // 4 - jnp.abs(phase - NRING // 2)
    x = quarter.astype(jnp.float32) * (2.0 * math.pi / NRING)
    y = x * x
    series = 0.0
    for power in (11, 9, 7, 5, 3):
        series = (series + (-1.0) ** (power // 2) / math.factorial(power)) * y
    return 1.0 - 0.5 * (x + x * series)


def params(mib):
    return pltpu.CompilerParams(vmem_limit_bytes=mib * MIB)


def parts(value):
    high = value.astype(jnp.bfloat16)
    return high, (value - high.astype(jnp.float32)).astype(jnp.bfloat16)


def product(left, right):
    terms = [(left[0], right[0]), (left[0], right[1]), (left[1], right[0])]
    done = [jnp.dot(x, y, preferred_element_type=jnp.float32) for x, y in terms]
    return done[0] + (done[1] + done[2])


def both_sides(h_a, block, h_b):
    return product(parts(product(h_a, parts(block))), h_b)


def send_coded(blocks, out_ref, copies):
    top = jnp.max(jnp.abs(blocks[0]))
    for block in blocks[1:]:
        top = jnp.maximum(top, jnp.max(jnp.abs(block)))
    exponent = jnp.ceil(jnp.log(jnp.full((TAIL, B), jnp.maximum(top, 1e-36))) * (FINE / LN2) + 0.125)
    gain = jnp.exp(exponent[:1] * (-LN2 / FINE))
    for at, block in enumerate(blocks):
        root = jnp.sqrt(jnp.sqrt(jnp.abs(block) * gain)) * CODES
        code = jnp.round(jnp.where(block < 0, -root, root)).astype(jnp.int32).astype(jnp.int16)
        for to in range(copies):
            out_ref[to, at * A : (at + 1) * A, :] = code
    scale = exponent.astype(jnp.int32).astype(jnp.int16)
    for to in range(copies):
        out_ref[to, len(blocks) * A :, :] = scale


def received(ref, source, at):
    rows = ref.shape[1]
    tail = ref[source, rows - TAIL : rows, :].astype(jnp.int32).astype(jnp.float32)[:1]
    gain = jnp.exp(tail * (LN2 / FINE))
    root = ref[source, at * A : (at + 1) * A, :].astype(jnp.int32).astype(jnp.float32) * (1.0 / CODES)
    return (root * jnp.abs(root)) * (root * root) * gain


def partner(lead, step, sign):
    z = (lead // 2 + LIMBS + sign * step[0]) % (LIMBS // 2)
    return z * 2 + (lead + step[1]) % 2


def inverse_kernel(lead_ref, exp_ref, cipher_ref, ha_ref, hb_ref, out_ref, x_ref):
    def spread(step, _):
        for at in (step * 16, step * 16 + 8):
            for limb in range(JS - 1):
                rows = [cipher_ref[0, limb, 1:2, pl.ds(pl.multiple_of((at + k) * B, B), B)] for k in range(8)]
                x_ref[limb, pl.ds(pl.multiple_of(at, 8), 8), :] = jnp.concatenate(rows, axis=0)
        return 0

    lax.fori_loop(0, A // 16, spread, 0)
    h_a, h_b = parts(ha_ref[...]), parts(hb_ref[...])
    done = []
    for limb in range(JS - 1):
        tw = twiddle(exp_ref[lead_ref[0] * (JS - 1) + limb])
        done.append(both_sides(h_a, x_ref[limb], h_b) / tw)
    send_coded(done, out_ref, 1)


def pack_kernel(km_ref, ks_ref, dm_ref, ds_ref, out_ref, rows_ref):
    for p in range(2):
        for digit in range(DNUM):
            at = p * 16 + digit * JS
            rows_ref[at : at + JS - 1, :] = km_ref[0, p, digit].astype(jnp.float32)
            rows_ref[at + JS - 1 : at + JS, :] = ks_ref[0, p, digit].astype(jnp.float32)
        at = p * 16 + DNUM * JS
        rows_ref[at : at + JS - 1, :] = dm_ref[0].astype(jnp.float32)
        rows_ref[at + JS - 1 : at + JS, :] = ds_ref[0].astype(jnp.float32)
    out_ref[...] = rows_ref[...].astype(jnp.bfloat16)


def combine(block, keys_ref, lanes_of, before_ref, sum_ref):
    sub = lax.broadcasted_iota(jnp.int32, (8, 128), 0)
    low_half = sub < JS
    base_gain = jnp.where((sub >= JS) & (sub < 2 * JS - 1), 1.0, 0.0).astype(jnp.float32)
    special = [[[], []], [[], []]]
    turned = block.T
    for g in range(8):
        lanes = lanes_of(g)
        keys = keys_ref[:, lanes].astype(jnp.float32)
        upper = turned[g * 16 : g * 16 + 8]
        lower = turned[g * 16 + 8 : g * 16 + 16]
        tail = keys[8:16]
        diag = jnp.where(low_half, jnp.roll(tail, JS, axis=0), tail)
        folded = []
        for p in range(2):
            gain = jnp.where(low_half, keys[p * 16 + 8 : p * 16 + 16], base_gain if p == 0 else 0.0)
            term = diag * (keys[p * 16 : p * 16 + 8] * upper + gain * lower)
            folded.append(term + jnp.roll(term, JS, axis=0))
        both = jnp.where(low_half, folded[0], folded[1])
        if before_ref is not None:
            both = both + before_ref[:, lanes]
        sum_ref[:, lanes] = both
        for p in range(2):
            special[p][g % 2].append(both[p * JS + JS - 1 : p * JS + JS])
    return special


def extend_kernel(
    lead_ref, exp_ref, up_ref, idx_ref, base_ref, ha_ref, hb_ref, keys_ref, *rest,
):
    held, (sum_ref, got_ref, coef_ref, raised_ref, rows_ref, turns_ref, ext_ref, *rest) = rest[:LIMBS], rest[LIMBS:]
    slots, got, arrive = rest[:SLOTS], rest[SLOTS : 2 * SLOTS], rest[-1]
    chunks = ROTS * NRING // LINE

    def fetch(chunk, slot):
        place = pl.ds(pl.multiple_of(chunk * LINE, LINE), LINE)
        return pltpu.make_async_copy(idx_ref.at[place], slots[slot], arrive.at[slot])

    for slot in range(SLOTS):
        fetch(slot, slot).start()
    lead = lead_ref[0]
    for step, held_ref in zip(STEPS, held):
        source = partner(lead, step, -1)
        for limb in range(JS - 1):
            coef_ref[source * (JS - 1) + limb] = received(held_ref, 0, limb)

    def lift(step, _):
        rows = pl.ds(pl.multiple_of(step * CHUNK, CHUNK), CHUNK)
        for digit in range(DNUM):
            limbs = range(digit * LIMBS, (digit + 1) * LIMBS)
            parts = [coef_ref[limb, rows, :] for limb in limbs]
            for j in range(JS):
                m = lead * (JS - 1) + j if j < JS - 1 else LIMBS * (JS - 1) + lead
                total = None
                for limb, part in zip(limbs, parts):
                    term = up_ref[limb, m] * part
                    total = term if total is None else total + term
                raised_ref[digit * JS + j, rows, :] = total
        return 0

    lax.fori_loop(0, LIMBS, lift, 0)

    h_a, h_b = parts(ha_ref[...]), parts(hb_ref[...])
    for j in range(JS):
        tw = twiddle(exp_ref[lead * (JS - 1) + j if j < JS - 1 else LIMBS * (JS - 1) + lead])
        for digit in range(DNUM):
            ch = digit * JS + j
            done = both_sides(h_a, raised_ref[ch] * tw, h_b)
            rows_ref[0, pl.ds(ch, A, stride=16), :] = done[:, :128]
            rows_ref[1, pl.ds(ch, A, stride=16), :] = done[:, 128:]

    def first(step, _):
        for k in range(8):
            i, half = step * 4 + k // 2, k % 2
            lanes = pl.ds(pl.multiple_of(i * B + half * 128, 128), 128)
            lines = [base_ref[0, limb, 0:1, lanes] for limb in range(JS - 1)] + [jnp.zeros((1, 128), jnp.float32)]
            rows_ref[half, pl.ds(pl.multiple_of(i * 16 + 8, 8) + 4, 4), :] = jnp.concatenate(lines, axis=0)
        return 0

    lax.fori_loop(0, A // 4, first, 0)

    source = lax.broadcasted_iota(jnp.int32, (2 * 128, 128), 0) & 127
    target = lax.broadcasted_iota(jnp.int32, (2 * 128, 128), 1)
    for by in range(8):
        ones = jnp.where(((source + by * 16) & 127) == target, 1.0, 0.0)
        turns_ref[:, by * 128 : (by + 1) * 128] = ones.astype(jnp.bfloat16)

    def turn(step, _):
        for k in range(4):
            at = pl.ds(pl.multiple_of(step * 256 + k // 2 * 128, 128), 128)
            both = jnp.concatenate(parts(rows_ref[k % 2, at, :].T), axis=1)
            turned = jnp.dot(both, turns_ref[...], preferred_element_type=jnp.float32)
            for by in range(8):
                at = pl.ds(pl.multiple_of(by * (NRING // 8) + step * (2 * B) + k * 128, 128), 128)
                ext_ref[at, :] = turned[:, by * 128 : (by + 1) * 128]
        return 0

    lax.fori_loop(0, A // 16, turn, 0)


    group = lax.broadcasted_iota(jnp.int32, (1, 128), 1) // 16

    def gather(chunk, slot, store):
        fetch(chunk, slot).wait()
        for r in range(128):
            row = None
            for g in range(8):
                one = ext_ref[pl.ds(slots[slot][g * 128 + r], 1), :]
                row = one if row is None else jnp.where(group == g, one, row)
            store(r, row)

    def own(step, _):
        def product_of(chunk, slot):
            lanes_of = lambda g: pl.ds(pl.multiple_of(chunk * LINE + g * 128, 128), 128)
            combine(got[slot][...], keys_ref, lanes_of, None, sum_ref)

        for slot in range(SLOTS):
            chunk = step * SLOTS + slot

            def store(r, row, slot=slot):
                got[slot][r : r + 1, :] = row

            gather(chunk, slot, store)
            if slot > 0:
                product_of(chunk - 1, slot - 1)
            fetch(chunk + SLOTS, slot).start()
        product_of(step * SLOTS + SLOTS - 1, SLOTS - 1)
        return 0

    lax.fori_loop(0, chunks // 2 // SLOTS, own, 0)

    def other(step, _):
        for slot in range(SLOTS):
            chunk = step * SLOTS + slot

            def store(r, row, chunk=chunk):
                got_ref[chunk - chunks // 2, r : r + 1, :] = row

            gather(chunk, slot, store)
            fetch(jnp.minimum(chunk + SLOTS, chunks - 1), slot).start()
        return 0

    lax.fori_loop(chunks // 2 // SLOTS, chunks // SLOTS, other, 0)
    for slot in range(SLOTS):
        fetch(chunks - 1, slot).wait()


def combine_kernel(
    lead_ref, exp_ref, got_ref, ha_ref, hb_ref, keys_ref, before_ref, sum_ref, low_ref, spec_ref,
):
    step = pl.program_id(0)
    for pair in range(BLOCKS // 2):
        done = []
        for blk in (2 * pair, 2 * pair + 1):
            lanes_of = lambda g: slice(blk * LINE + g * 128, blk * LINE + g * 128 + 128)
            done.append(combine(got_ref[blk], keys_ref, lanes_of, before_ref, sum_ref))
        at = pl.ds(pl.multiple_of(step * (BLOCKS * 4) + pair * 8, 8), 8)
        for p in range(2):
            for half in range(2):
                eight = done[0][p][half] + done[1][p][half]
                spec_ref[p, at, half * 128 : (half + 1) * 128] = jnp.concatenate(eight, axis=0)

    @pl.when(step == pl.num_programs(0) - 1)
    def _():
        tw = twiddle(exp_ref[LIMBS * (JS - 1) + lead_ref[0]])
        h_a, h_b = parts(ha_ref[...]), parts(hb_ref[...])
        send_coded([both_sides(h_a, spec_ref[p], h_b) / tw for p in range(2)], low_ref, LIMBS)


def finish_kernel(lead_ref, exp_ref, down_ref, sum_ref, ha_ref, hb_ref, held_ref, out_ref, low_ref, returned_ref, rows_ref):
    lead = lead_ref[0]
    h_a, h_b = parts(ha_ref[...]), parts(hb_ref[...])
    for source in range(LIMBS):
        for p in range(2):
            low_ref[source * 2 + p] = received(held_ref, source, p)

    def lower(step, _):
        rows = pl.ds(pl.multiple_of(step * CHUNK, CHUNK), CHUNK)
        for p in range(2):
            parts = [low_ref[k * 2 + p, rows, :] for k in range(LIMBS)]
            for j in range(JS - 1):
                total = None
                for k, part in enumerate(parts):
                    term = down_ref[k, lead * (JS - 1) + j] * part
                    total = term if total is None else total + term
                returned_ref[p * (JS - 1) + j, rows, :] = total
        return 0

    lax.fori_loop(0, LIMBS, lower, 0)
    for j in range(JS - 1):
        tw = twiddle(exp_ref[lead * (JS - 1) + j])
        for p in range(2):
            done = both_sides(h_a, returned_ref[p * (JS - 1) + j] * tw, h_b)
            rows_ref[0, pl.ds(p * JS + j, A, stride=8), :] = done[:, :128]
            rows_ref[1, pl.ds(p * JS + j, A, stride=8), :] = done[:, 128:]

    def body(step, _):
        for k in range(8):
            i, half = step * 4 + k // 2, k % 2
            lanes = pl.ds(pl.multiple_of(i * B + half * 128, 128), 128)
            left = sum_ref[:, lanes] - rows_ref[half, pl.ds(pl.multiple_of(i * 8, 8), 8), :]
            for j in range(JS - 1):
                out_ref[0, j, :, lanes] = jnp.concatenate([left[j : j + 1], left[JS + j : JS + j + 1]], axis=0)
        return 0

    lax.fori_loop(0, A // 4, body, 0)


def exchange(value):
    return lax.all_to_all(value, "limb", split_axis=0, concat_axis=0, tiled=True)


def rows_of(perms):
    place = jnp.arange(perms.shape[0], dtype=jnp.int32) >> 7
    by = (place - (perms >> 8)) & 7
    return (by << 12) + ((perms >> 11) << 8) + (perms & (B - 1))


def f32(*shape):
    return jax.ShapeDtypeStruct(shape, jnp.float32)


def cost(micros):
    return pl.CostEstimate(flops=int(micros * 1e9), bytes_accessed=1 << 20, transcendentals=0)


def on_device(cipher, key_main, key_special, diag_main, diag_special, perms, tw_exp, up_conv, down_conv):
    lead = lax.axis_index("limb").astype(jnp.int32)[None]
    h_a, h_b = jnp.asarray(hartley(A)), jnp.asarray(hartley(B))
    cipher = cipher.transpose(0, 2, 1, 3)

    coefs = pl.pallas_call(
        inverse_kernel,
        out_shape=jax.ShapeDtypeStruct((1, (JS - 1) * A + TAIL, B), jnp.int16),
        in_specs=[SMEM, SMEM, VMEM, VMEM, VMEM],
        out_specs=VMEM,
        scratch_shapes=[pltpu.VMEM((JS - 1, A, B), jnp.float32)],
        compiler_params=params(60),
        cost_estimate=cost(2),
        name="coefficients",
    )(lead, tw_exp, cipher, h_a, h_b)
    held = [coefs] + [
        lax.ppermute(coefs, "limb", [(source, partner(source, step, 1)) for source in range(LIMBS)])
        for step in STEPS[1:]
    ]

    count = lax.axis_size("key")
    ahead = [((target + 1) % count, target) for target in range(count)]
    key_main, key_special, diag_main, diag_special, perm_own, held[-1] = lax.optimization_barrier(
        (key_main, key_special, diag_main, diag_special, perms[0], held[-1])
    )
    lanes = NRING // 4
    packed = pl.pallas_call(
        pack_kernel,
        grid=(4,),
        out_shape=jax.ShapeDtypeStruct((32, NRING), jnp.bfloat16),
        in_specs=[
            pl.BlockSpec((1, 2, DNUM, JS - 1, lanes), lambda step: (0, 0, 0, 0, step)),
            pl.BlockSpec((1, 2, DNUM, 1, lanes), lambda step: (0, 0, 0, 0, step)),
            pl.BlockSpec((1, JS - 1, lanes), lambda step: (0, 0, step)),
            pl.BlockSpec((1, 1, lanes), lambda step: (0, 0, step)),
        ],
        out_specs=pl.BlockSpec((32, lanes), lambda step: (0, step)),
        scratch_shapes=[pltpu.VMEM((32, lanes), jnp.float32)],
        compiler_params=params(32),
        cost_estimate=cost(2),
        name="pack_keys",
    )(key_main, key_special, diag_main, diag_special)
    both_rows = rows_of(jnp.concatenate([perm_own, lax.ppermute(perm_own, "key", ahead)]))
    packed, both_rows, *held = lax.optimization_barrier((packed, both_rows, *held))
    packed_next = lax.ppermute(packed, "key", ahead)

    half_lines = NRING // LINE
    first, gathered = pl.pallas_call(
        extend_kernel,
        out_shape=(f32(2 * JS, NRING), f32(half_lines, 128, 128)),
        in_specs=[SMEM] * 3 + [pl.BlockSpec(memory_space=pl.ANY)] + [VMEM] * (4 + LIMBS),
        out_specs=(VMEM, VMEM),
        scratch_shapes=[
            pltpu.VMEM((LIMBS * (JS - 1), A, B), jnp.float32),
            pltpu.VMEM((DNUM * JS, A, B), jnp.float32),
            pltpu.VMEM((2, A * 16, 128), jnp.float32),
            pltpu.VMEM((2 * 128, 8 * 128), jnp.bfloat16),
            pltpu.VMEM((NRING, 128), jnp.float32),
        ]
        + [pltpu.SMEM((LINE,), jnp.int32)] * SLOTS
        + [pltpu.VMEM((128, 128), jnp.float32)] * SLOTS
        + [pltpu.SemaphoreType.DMA((SLOTS,))],
        compiler_params=params(40),
        cost_estimate=cost(50),
        name="extend_and_gather",
    )(lead, tw_exp, up_conv, both_rows, cipher, h_a, h_b, packed, *held)

    lines = (BLOCKS, 128, 128)
    columns = pl.BlockSpec((2 * JS, BLOCKS * LINE), lambda step: (0, step))
    low_shape = (LIMBS, 2 * A + TAIL, B)
    summed, lowered = pl.pallas_call(
        combine_kernel,
        grid=(half_lines // BLOCKS,),
        out_shape=(f32(2 * JS, NRING), jax.ShapeDtypeStruct(low_shape, jnp.int16)),
        in_specs=[SMEM] * 2
        + [
            pl.BlockSpec(lines, lambda step: (step, 0, 0)),
            pl.BlockSpec((A, A), lambda step: (0, 0)),
            pl.BlockSpec((B, B), lambda step: (0, 0)),
            pl.BlockSpec((32, BLOCKS * LINE), lambda step: (0, step)),
            columns,
        ],
        out_specs=(columns, pl.BlockSpec(low_shape, lambda step: (0, 0, 0))),
        scratch_shapes=[pltpu.VMEM((2, A, B), jnp.float32)],
        compiler_params=params(32),
        cost_estimate=cost(4),
        name="switch_next",
    )(lead, tw_exp, gathered, h_a, h_b, packed_next, first)
    special = exchange(lowered)

    result = pl.pallas_call(
        finish_kernel,
        out_shape=f32(1, JS - 1, 2, NRING),
        in_specs=[SMEM] * 3 + [VMEM] * 4,
        out_specs=VMEM,
        scratch_shapes=[
            pltpu.VMEM((LIMBS * 2, A, B), jnp.float32),
            pltpu.VMEM((2 * (JS - 1), A, B), jnp.float32),
            pltpu.VMEM((2, A * 8, 128), jnp.float32),
        ],
        compiler_params=params(60),
        cost_estimate=cost(4),
        name="finish",
    )(lead, tw_exp, down_conv, summed, h_a, h_b, special)
    return result.transpose(0, 2, 1, 3)


def solution(mesh):
    placed = (
        P("key", None, "limb", None),
        P("key", None, None, "limb", None),
        P("key", None, None, "limb", None),
        P("key", "limb", None),
        P("key", "limb", None),
        P("key", None),
        P(),
        P(),
        P(),
    )
    return jax.shard_map(
        on_device,
        mesh=mesh,
        in_specs=placed,
        out_specs=P("key", None, "limb", None),
        check_vma=False,
    )
```

```python
import functools
import math

import jax
import jax.numpy as jnp
import numpy as np
from jax import lax
from jax.experimental import pallas as pl
from jax.experimental.pallas import tpu as pltpu
from jax.sharding import PartitionSpec as P

A = 128
B = 256
NRING = A * B
DNUM = 3
LIMBS = 8
JS = 4
CHUNK = A // LIMBS
HIGHEST = lax.Precision.HIGHEST
MIB = 1 << 20
LN2 = math.log(2.0)
LINE = 1024
SLOTS = 4
STEPS = ((0, 0), (3, 0), (1, 0), (0, 1), (2, 0), (3, 1), (1, 1), (2, 1))
BLOCKS = 4
ROTS = 2
TAIL = 16
FINE = 16
CODES = 32767.0

VMEM = pl.BlockSpec(memory_space=pltpu.VMEM)
SMEM = pl.BlockSpec(memory_space=pltpu.SMEM)


def hartley(extent):
    indices = np.arange(extent)
    angles = (indices[:, None] * indices[None, :] % extent) * (2.0 * math.pi / extent)
    return ((np.cos(angles) + np.sin(angles)) / math.sqrt(extent)).astype(np.float32)


def twiddle(exponent):
    product = lax.broadcasted_iota(jnp.int32, (A, B), 0) * lax.broadcasted_iota(jnp.int32, (A, B), 1)
    phase = ((product & (NRING - 1)) * exponent) & (NRING - 1)
    quarter = NRING // 4 - jnp.abs(phase - NRING // 2)
    x = quarter.astype(jnp.float32) * (2.0 * math.pi / NRING)
    y = x * x
    series = 0.0
    for power in (11, 9, 7, 5, 3):
        series = (series + (-1.0) ** (power // 2) / math.factorial(power)) * y
    return 1.0 - 0.5 * (x + x * series)


def params(mib):
    return pltpu.CompilerParams(vmem_limit_bytes=mib * MIB)


def parts(value):
    high = value.astype(jnp.bfloat16)
    return high, (value - high.astype(jnp.float32)).astype(jnp.bfloat16)


def product(left, right):
    terms = [(left[0], right[0]), (left[0], right[1]), (left[1], right[0])]
    done = [jnp.dot(x, y, preferred_element_type=jnp.float32) for x, y in terms]
    return done[0] + (done[1] + done[2])


def both_sides(h_a, block, h_b):
    return product(parts(product(h_a, parts(block))), h_b)


def send_coded(blocks, out_ref):
    top = jnp.max(jnp.abs(blocks[0]))
    for block in blocks[1:]:
        top = jnp.maximum(top, jnp.max(jnp.abs(block)))
    exponent = jnp.ceil(jnp.log(jnp.full((TAIL, B), jnp.maximum(top, 1e-36))) * (FINE / LN2) + 0.125)
    gain = jnp.exp(exponent[:1] * (-LN2 / FINE))
    for at, block in enumerate(blocks):
        root = jnp.sqrt(jnp.sqrt(jnp.abs(block) * gain)) * CODES
        code = jnp.round(jnp.where(block < 0, -root, root)).astype(jnp.int32).astype(jnp.int16)
        out_ref[at * A : (at + 1) * A, :] = code
    out_ref[len(blocks) * A :, :] = exponent.astype(jnp.int32).astype(jnp.int16)


def received(ref, at):
    rows = ref.shape[0]
    tail = ref[rows - TAIL : rows, :].astype(jnp.int32).astype(jnp.float32)[:1]
    gain = jnp.exp(tail * (LN2 / FINE))
    root = ref[at * A : (at + 1) * A, :].astype(jnp.int32).astype(jnp.float32) * (1.0 / CODES)
    return (root * jnp.abs(root)) * (root * root) * gain


def partner(lead, step, sign):
    z = (lead // 2 + LIMBS + sign * step[0]) % (LIMBS // 2)
    return z * 2 + (lead + step[1]) % 2


def inverse_kernel(lead_ref, exp_ref, cipher_ref, ha_ref, hb_ref, out_ref, x_ref):
    def spread(step, _):
        for at in (step * 16, step * 16 + 8):
            for limb in range(JS - 1):
                rows = [cipher_ref[0, limb, 1:2, pl.ds(pl.multiple_of((at + k) * B, B), B)] for k in range(8)]
                x_ref[limb, pl.ds(pl.multiple_of(at, 8), 8), :] = jnp.concatenate(rows, axis=0)
        return 0

    lax.fori_loop(0, A // 16, spread, 0)
    h_a, h_b = parts(ha_ref[...]), parts(hb_ref[...])
    done = []
    for limb in range(JS - 1):
        tw = twiddle(exp_ref[lead_ref[0] * (JS - 1) + limb])
        done.append(both_sides(h_a, x_ref[limb], h_b) / tw)
    send_coded(done, out_ref)


def pack_kernel(km_ref, ks_ref, dm_ref, ds_ref, out_ref, rows_ref):
    for p in range(2):
        for digit in range(DNUM):
            at = p * 16 + digit * JS
            rows_ref[at : at + JS - 1, :] = km_ref[0, p, digit].astype(jnp.float32)
            rows_ref[at + JS - 1 : at + JS, :] = ks_ref[0, p, digit].astype(jnp.float32)
        at = p * 16 + DNUM * JS
        rows_ref[at : at + JS - 1, :] = dm_ref[0].astype(jnp.float32)
        rows_ref[at + JS - 1 : at + JS, :] = ds_ref[0].astype(jnp.float32)
    out_ref[...] = rows_ref[...].astype(jnp.bfloat16)


def combine(block, keys_ref, lanes_of, before_ref, sum_ref):
    sub = lax.broadcasted_iota(jnp.int32, (8, 128), 0)
    low_half = sub < JS
    base_gain = jnp.where((sub >= JS) & (sub < 2 * JS - 1), 1.0, 0.0).astype(jnp.float32)
    special = [[[], []], [[], []]]
    turned = block.T
    for g in range(8):
        lanes = lanes_of(g)
        keys = keys_ref[:, lanes].astype(jnp.float32)
        upper = turned[g * 16 : g * 16 + 8]
        lower = turned[g * 16 + 8 : g * 16 + 16]
        tail = keys[8:16]
        diag = jnp.where(low_half, jnp.roll(tail, JS, axis=0), tail)
        folded = []
        for p in range(2):
            gain = jnp.where(low_half, keys[p * 16 + 8 : p * 16 + 16], base_gain if p == 0 else 0.0)
            term = diag * (keys[p * 16 : p * 16 + 8] * upper + gain * lower)
            folded.append(term + jnp.roll(term, JS, axis=0))
        both = jnp.where(low_half, folded[0], folded[1])
        if before_ref is not None:
            both = both + before_ref[:, lanes]
        sum_ref[:, lanes] = both
        for p in range(2):
            special[p][g % 2].append(both[p * JS + JS - 1 : p * JS + JS])
    return special


def extend_kernel(
    lead_ref, exp_ref, up_ref, idx_ref, base_ref, ha_ref, hb_ref, keys_ref, *rest,
):
    held, (sum_ref, got_ref, coef_ref, raised_ref, rows_ref, turns_ref, ext_ref, *rest) = rest[:LIMBS], rest[LIMBS:]
    slots, got, arrive = rest[:SLOTS], rest[SLOTS : 2 * SLOTS], rest[-1]
    chunks = ROTS * NRING // LINE

    def fetch(chunk, slot):
        place = pl.ds(pl.multiple_of(chunk * LINE, LINE), LINE)
        return pltpu.make_async_copy(idx_ref.at[place], slots[slot], arrive.at[slot])

    for slot in range(SLOTS):
        fetch(slot, slot).start()
    lead = lead_ref[0]
    for step, held_ref in zip(STEPS, held):
        source = partner(lead, step, -1)
        for limb in range(JS - 1):
            coef_ref[source * (JS - 1) + limb] = received(held_ref, limb)

    def lift(step, _):
        rows = pl.ds(pl.multiple_of(step * CHUNK, CHUNK), CHUNK)
        for digit in range(DNUM):
            limbs = range(digit * LIMBS, (digit + 1) * LIMBS)
            parts = [coef_ref[limb, rows, :] for limb in limbs]
            for j in range(JS):
                m = lead * (JS - 1) + j if j < JS - 1 else LIMBS * (JS - 1) + lead
                total = None
                for limb, part in zip(limbs, parts):
                    term = up_ref[limb, m] * part
                    total = term if total is None else total + term
                raised_ref[digit * JS + j, rows, :] = total
        return 0

    lax.fori_loop(0, LIMBS, lift, 0)

    h_a, h_b = parts(ha_ref[...]), parts(hb_ref[...])
    for j in range(JS):
        tw = twiddle(exp_ref[lead * (JS - 1) + j if j < JS - 1 else LIMBS * (JS - 1) + lead])
        for digit in range(DNUM):
            ch = digit * JS + j
            done = both_sides(h_a, raised_ref[ch] * tw, h_b)
            rows_ref[0, pl.ds(ch, A, stride=16), :] = done[:, :128]
            rows_ref[1, pl.ds(ch, A, stride=16), :] = done[:, 128:]

    def first(step, _):
        for k in range(8):
            i, half = step * 4 + k // 2, k % 2
            lanes = pl.ds(pl.multiple_of(i * B + half * 128, 128), 128)
            lines = [base_ref[0, limb, 0:1, lanes] for limb in range(JS - 1)] + [jnp.zeros((1, 128), jnp.float32)]
            rows_ref[half, pl.ds(pl.multiple_of(i * 16 + 8, 8) + 4, 4), :] = jnp.concatenate(lines, axis=0)
        return 0

    lax.fori_loop(0, A // 4, first, 0)

    source = lax.broadcasted_iota(jnp.int32, (2 * 128, 128), 0) & 127
    target = lax.broadcasted_iota(jnp.int32, (2 * 128, 128), 1)
    for by in range(8):
        ones = jnp.where(((source + by * 16) & 127) == target, 1.0, 0.0)
        turns_ref[:, by * 128 : (by + 1) * 128] = ones.astype(jnp.bfloat16)

    def turn(step, _):
        for k in range(8):
            at = pl.ds(pl.multiple_of(step * 512 + k // 2 * 128, 128), 128)
            both = jnp.concatenate(parts(rows_ref[k % 2, at, :].T), axis=1)
            turned = jnp.dot(both, turns_ref[...], preferred_element_type=jnp.float32)
            for by in range(8):
                at = pl.ds(pl.multiple_of(by * (NRING // 8) + step * (4 * B) + k * 128, 128), 128)
                ext_ref[at, :] = turned[:, by * 128 : (by + 1) * 128]
        return 0

    lax.fori_loop(0, A // 32, turn, 0)


    group = lax.broadcasted_iota(jnp.int32, (1, 128), 1) // 16

    def gather(chunk, slot, store):
        fetch(chunk, slot).wait()
        for r in range(128):
            row = None
            for g in range(8):
                one = ext_ref[pl.ds(slots[slot][g * 128 + r], 1), :]
                row = one if row is None else jnp.where(group == g, one, row)
            store(r, row)

    def own(step, _):
        def product_of(chunk, slot):
            lanes_of = lambda g: pl.ds(pl.multiple_of(chunk * LINE + g * 128, 128), 128)
            combine(got[slot][...], keys_ref, lanes_of, None, sum_ref)

        for slot in range(SLOTS):
            chunk = step * SLOTS + slot

            def store(r, row, slot=slot):
                got[slot][r : r + 1, :] = row

            gather(chunk, slot, store)
            if slot > 0:
                product_of(chunk - 1, slot - 1)
            fetch(chunk + SLOTS, slot).start()
        product_of(step * SLOTS + SLOTS - 1, SLOTS - 1)
        return 0

    lax.fori_loop(0, chunks // 2 // SLOTS, own, 0)

    def other(step, _):
        for slot in range(SLOTS):
            chunk = step * SLOTS + slot

            def store(r, row, chunk=chunk):
                got_ref[chunk - chunks // 2, r : r + 1, :] = row

            gather(chunk, slot, store)
            fetch(jnp.minimum(chunk + SLOTS, chunks - 1), slot).start()
        return 0

    lax.fori_loop(chunks // 2 // SLOTS, chunks // SLOTS, other, 0)
    for slot in range(SLOTS):
        fetch(chunks - 1, slot).wait()


def combine_kernel(
    lead_ref, exp_ref, got_ref, ha_ref, hb_ref, keys_ref, before_ref, sum_ref, low_ref, spec_ref,
):
    step = pl.program_id(0)
    for pair in range(BLOCKS // 2):
        done = []
        for blk in (2 * pair, 2 * pair + 1):
            lanes_of = lambda g: slice(blk * LINE + g * 128, blk * LINE + g * 128 + 128)
            done.append(combine(got_ref[blk], keys_ref, lanes_of, before_ref, sum_ref))
        at = pl.ds(pl.multiple_of(step * (BLOCKS * 4) + pair * 8, 8), 8)
        for p in range(2):
            for half in range(2):
                eight = done[0][p][half] + done[1][p][half]
                spec_ref[p, at, half * 128 : (half + 1) * 128] = jnp.concatenate(eight, axis=0)

    @pl.when(step == pl.num_programs(0) - 1)
    def _():
        tw = twiddle(exp_ref[LIMBS * (JS - 1) + lead_ref[0]])
        h_a, h_b = parts(ha_ref[...]), parts(hb_ref[...])
        send_coded([both_sides(h_a, spec_ref[p], h_b) / tw for p in range(2)], low_ref)


def finish_kernel(lead_ref, exp_ref, down_ref, sum_ref, ha_ref, hb_ref, *rest):
    held, (out_ref, low_ref, returned_ref, rows_ref) = rest[:LIMBS], rest[LIMBS:]
    lead = lead_ref[0]
    h_a, h_b = parts(ha_ref[...]), parts(hb_ref[...])
    for step, held_ref in zip(STEPS, held):
        source = partner(lead, step, -1)
        for p in range(2):
            low_ref[source * 2 + p] = received(held_ref, p)

    def lower(step, _):
        rows = pl.ds(pl.multiple_of(step * CHUNK, CHUNK), CHUNK)
        for p in range(2):
            parts = [low_ref[k * 2 + p, rows, :] for k in range(LIMBS)]
            for j in range(JS - 1):
                total = None
                for k, part in enumerate(parts):
                    term = down_ref[k, lead * (JS - 1) + j] * part
                    total = term if total is None else total + term
                returned_ref[p * (JS - 1) + j, rows, :] = total
        return 0

    lax.fori_loop(0, LIMBS, lower, 0)
    for j in range(JS - 1):
        tw = twiddle(exp_ref[lead * (JS - 1) + j])
        for p in range(2):
            done = both_sides(h_a, returned_ref[p * (JS - 1) + j] * tw, h_b)
            rows_ref[0, pl.ds(p * JS + j, A, stride=8), :] = done[:, :128]
            rows_ref[1, pl.ds(p * JS + j, A, stride=8), :] = done[:, 128:]

    def body(step, _):
        for k in range(8):
            i, half = step * 4 + k // 2, k % 2
            lanes = pl.ds(pl.multiple_of(i * B + half * 128, 128), 128)
            left = sum_ref[:, lanes] - rows_ref[half, pl.ds(pl.multiple_of(i * 8, 8), 8), :]
            for j in range(JS - 1):
                out_ref[0, j, :, lanes] = jnp.concatenate([left[j : j + 1], left[JS + j : JS + j + 1]], axis=0)
        return 0

    lax.fori_loop(0, A // 4, body, 0)


def spread_limbs(value):
    return [value] + [
        lax.ppermute(value, "limb", [(source, partner(source, step, 1)) for source in range(LIMBS)])
        for step in STEPS[1:]
    ]


def rows_of(perms):
    place = jnp.arange(perms.shape[0], dtype=jnp.int32) >> 7
    by = (place - (perms >> 8)) & 7
    return (by << 12) + ((perms >> 11) << 8) + (perms & (B - 1))


def f32(*shape):
    return jax.ShapeDtypeStruct(shape, jnp.float32)


def cost(micros):
    return pl.CostEstimate(flops=int(micros * 1e9), bytes_accessed=1 << 20, transcendentals=0)


def on_device(cipher, key_main, key_special, diag_main, diag_special, perms, tw_exp, up_conv, down_conv):
    lead = lax.axis_index("limb").astype(jnp.int32)[None]
    h_a, h_b = jnp.asarray(hartley(A)), jnp.asarray(hartley(B))
    cipher = cipher.transpose(0, 2, 1, 3)

    coefs = pl.pallas_call(
        inverse_kernel,
        out_shape=jax.ShapeDtypeStruct(((JS - 1) * A + TAIL, B), jnp.int16),
        in_specs=[SMEM, SMEM, VMEM, VMEM, VMEM],
        out_specs=VMEM,
        scratch_shapes=[pltpu.VMEM((JS - 1, A, B), jnp.float32)],
        compiler_params=params(60),
        cost_estimate=cost(2),
        name="coefficients",
    )(lead, tw_exp, cipher, h_a, h_b)
    held = spread_limbs(coefs)

    count = lax.axis_size("key")
    ahead = [((target + 1) % count, target) for target in range(count)]
    key_main, key_special, diag_main, diag_special, perm_own, held[-1] = lax.optimization_barrier(
        (key_main, key_special, diag_main, diag_special, perms[0], held[-1])
    )
    lanes = NRING // 4
    packed = pl.pallas_call(
        pack_kernel,
        grid=(4,),
        out_shape=jax.ShapeDtypeStruct((32, NRING), jnp.bfloat16),
        in_specs=[
            pl.BlockSpec((1, 2, DNUM, JS - 1, lanes), lambda step: (0, 0, 0, 0, step)),
            pl.BlockSpec((1, 2, DNUM, 1, lanes), lambda step: (0, 0, 0, 0, step)),
            pl.BlockSpec((1, JS - 1, lanes), lambda step: (0, 0, step)),
            pl.BlockSpec((1, 1, lanes), lambda step: (0, 0, step)),
        ],
        out_specs=pl.BlockSpec((32, lanes), lambda step: (0, step)),
        scratch_shapes=[pltpu.VMEM((32, lanes), jnp.float32)],
        compiler_params=params(32),
        cost_estimate=cost(2),
        name="pack_keys",
    )(key_main, key_special, diag_main, diag_special)
    both_rows = rows_of(jnp.concatenate([perm_own, lax.ppermute(perm_own, "key", ahead)]))
    packed, both_rows, *held = lax.optimization_barrier((packed, both_rows, *held))
    packed_next = lax.ppermute(packed, "key", ahead)

    half_lines = NRING // LINE
    first, gathered = pl.pallas_call(
        extend_kernel,
        out_shape=(f32(2 * JS, NRING), f32(half_lines, 128, 128)),
        in_specs=[SMEM] * 3 + [pl.BlockSpec(memory_space=pl.ANY)] + [VMEM] * (4 + LIMBS),
        out_specs=(VMEM, VMEM),
        scratch_shapes=[
            pltpu.VMEM((LIMBS * (JS - 1), A, B), jnp.float32),
            pltpu.VMEM((DNUM * JS, A, B), jnp.float32),
            pltpu.VMEM((2, A * 16, 128), jnp.float32),
            pltpu.VMEM((2 * 128, 8 * 128), jnp.bfloat16),
            pltpu.VMEM((NRING, 128), jnp.float32),
        ]
        + [pltpu.SMEM((LINE,), jnp.int32)] * SLOTS
        + [pltpu.VMEM((128, 128), jnp.float32)] * SLOTS
        + [pltpu.SemaphoreType.DMA((SLOTS,))],
        compiler_params=params(40),
        cost_estimate=cost(50),
        name="extend_and_gather",
    )(lead, tw_exp, up_conv, both_rows, cipher, h_a, h_b, packed, *held)

    lines = (BLOCKS, 128, 128)
    columns = pl.BlockSpec((2 * JS, BLOCKS * LINE), lambda step: (0, step))
    low_shape = (2 * A + TAIL, B)
    summed, lowered = pl.pallas_call(
        combine_kernel,
        grid=(half_lines // BLOCKS,),
        out_shape=(f32(2 * JS, NRING), jax.ShapeDtypeStruct(low_shape, jnp.int16)),
        in_specs=[SMEM] * 2
        + [
            pl.BlockSpec(lines, lambda step: (step, 0, 0)),
            pl.BlockSpec((A, A), lambda step: (0, 0)),
            pl.BlockSpec((B, B), lambda step: (0, 0)),
            pl.BlockSpec((32, BLOCKS * LINE), lambda step: (0, step)),
            columns,
        ],
        out_specs=(columns, pl.BlockSpec(low_shape, lambda step: (0, 0))),
        scratch_shapes=[pltpu.VMEM((2, A, B), jnp.float32)],
        compiler_params=params(32),
        cost_estimate=cost(4),
        name="switch_next",
    )(lead, tw_exp, gathered, h_a, h_b, packed_next, first)
    special = spread_limbs(lowered)

    result = pl.pallas_call(
        finish_kernel,
        out_shape=f32(1, JS - 1, 2, NRING),
        in_specs=[SMEM] * 3 + [VMEM] * (3 + LIMBS),
        out_specs=VMEM,
        scratch_shapes=[
            pltpu.VMEM((LIMBS * 2, A, B), jnp.float32),
            pltpu.VMEM((2 * (JS - 1), A, B), jnp.float32),
            pltpu.VMEM((2, A * 8, 128), jnp.float32),
        ],
        compiler_params=params(60),
        cost_estimate=cost(4),
        name="finish",
    )(lead, tw_exp, down_conv, summed, h_a, h_b, *special)
    return result.transpose(0, 2, 1, 3)


def solution(mesh):
    placed = (
        P("key", None, "limb", None),
        P("key", None, None, "limb", None),
        P("key", None, None, "limb", None),
        P("key", "limb", None),
        P("key", "limb", None),
        P("key", None),
        P(),
        P(),
        P(),
    )
    return jax.shard_map(
        on_device,
        mesh=mesh,
        in_specs=placed,
        out_specs=P("key", None, "limb", None),
        check_vma=False,
    )
```
